256 devices in a mesh: cfg: 2 (over z_lo), seq: 128 (over x, z_hi, y, core).
Axes of the slice: x: 4, y: 4, z: 8 (z_hi: 4, z_lo: 2; z = z_hi * 2 + z_lo), core: 2. Of those that a mesh axis runs over, the one named last changes fastest.
Arguments:
- video_hidden: bfloat16 [2, 8192, 3072], P('cfg', 'seq'), may hold values from -6 to 6
- video_weight: bfloat16 [3072, 1536], replicated, may hold values from -0.109375 to 0.109375
- video_key: bfloat16 [2, 8192, 1536], P('cfg', 'seq'), may hold values from -6 to 6
- video_value: bfloat16 [2, 8192, 1536], P('cfg', 'seq'), may hold values from -6 to 6
- audio_cross_key: bfloat16 [2, 1024, 1536], P('cfg', 'seq'), may hold values from -6 to 6
- audio_cross_value: bfloat16 [2, 1024, 1536], P('cfg', 'seq'), may hold values from -6 to 6
- audio_query: bfloat16 [2, 1024, 1536], P('cfg', 'seq'), may hold values from -6 to 6
- audio_self_query: bfloat16 [2, 1024, 1536], P('cfg', 'seq'), may hold values from -6 to 6
- audio_self_key: bfloat16 [2, 1024, 1536], P('cfg', 'seq'), may hold values from -6 to 6
- audio_self_value: bfloat16 [2, 1024, 1536], P('cfg', 'seq'), may hold values from -6 to 6
- v2a_qgain: float32 [1536], replicated, may hold values from 0.1 to 1.9
- v2a_kgain: float32 [1536], replicated, may hold values from 0.1 to 1.9
- self_qgain: float32 [1536], replicated, may hold values from 0.1 to 1.9
- self_kgain: float32 [1536], replicated, may hold values from 0.1 to 1.9
- a2v_qgain: float32 [1536], replicated, may hold values from 0.1 to 1.9
- a2v_kgain: float32 [1536], replicated, may hold values from 0.1 to 1.9
- video_time: int32 [8192], P('seq'), may hold values from 0 to 2047
- audio_time: int32 [1024], P('seq'), may hold values from 0 to 2047
- branch_keep: int32 [2, 1024], P('cfg', 'seq'), may hold values from 0 to 1, as said below
Outputs:
- video_guided: bfloat16 [8192, 1536], P('seq', 'cfg')
- audio_guided: bfloat16 [1024, 1536], P('seq', 'cfg')
The draws below stay inside these ranges and needn't reach their ends.
Inputs may be any that keep to these rules, and one draw needn't show every extreme that they name: `branch_keep`: in each branch every audio token whose index is a multiple of 16 is kept.
All inputs are finite; a program needn't handle non-finite values.
Results may differ from the reference program's by a relative error of at most 0.0089.
Values may be sent and summed in bfloat16 or wider, within the bound.
A program may use at most 128 MiB of HBM per device.

```python
import math
import jax
import jax.numpy as jnp
from jax import lax

D = 3072
HEADS = 12
HEAD_DIM = 128
HW = 1536
VID_TOKENS = 8192
AUD_TOKENS = 1024


def draw_branch_keep(key, part):
    key = jax.random.fold_in(key, 7)
    sampled = jax.random.randint(key, (2, AUD_TOKENS), 0, 4)
    kept_draw = (sampled > 0).astype(jnp.int32)
    indices = jnp.arange(AUD_TOKENS, dtype=jnp.int32)
    forced = (indices % 16 == 0)[None, :]
    return jnp.where(forced, 1, kept_draw).astype(jnp.int32)


def with_ends(values, rng, low, high):
    place = [jax.random.randint(jax.random.fold_in(rng, axis), (), 0, length) for axis, length in enumerate(values.shape)]
    widest = values.shape.index(max(values.shape))
    beside = place[:widest] + [(place[widest] + 1) % values.shape[widest]] + place[widest + 1:]
    return values.at[tuple(place)].set(low).at[tuple(beside)].set(high)


def level_of(own_key, shape, shards, smallest, largest):
    gain, own = 1.0, jax.random.fold_in(own_key, 6)
    for dim, blocks in shards:
        heights = jnp.exp(jax.random.uniform(jax.random.fold_in(own, dim), (blocks,), jnp.float32, smallest / len(shards), largest / len(shards)))
        gain = gain * jnp.repeat(heights, shape[dim] // blocks).reshape([-1 if axis == dim else 1 for axis in range(len(shape))])
    return gain


def centred(own_key, extent, width, limit, cuts=(), kind=jnp.bfloat16):
    entries = jax.random.normal(own_key, extent, jnp.float32) * width
    if len(cuts) > 0:
        entries = level_of(own_key, extent, cuts, -0.22, 0.18) * entries
    return jnp.clip(entries, min=-limit, max=limit).astype(kind)


def setup_inputs(seed: int = 0) -> dict:
    key_of = jax.random.split(jax.random.key(seed), 20)
    return {
        "video_hidden": centred(key_of[0], (2, VID_TOKENS, D), 1.0, 6.0, ((0, 2), (1, 128))),
        "video_weight": centred(key_of[1], (D, HW), D ** -0.5, 0.109375),
        "video_key": centred(key_of[2], (2, VID_TOKENS, HW), 1.0, 6.0, ((0, 2), (1, 128))),
        "video_value": centred(key_of[3], (2, VID_TOKENS, HW), 1.0, 6.0, ((0, 2), (1, 128))),
        "audio_cross_key": centred(key_of[4], (2, AUD_TOKENS, HW), 1.0, 6.0, ((0, 2), (1, 128))),
        "audio_cross_value": centred(key_of[5], (2, AUD_TOKENS, HW), 1.0, 6.0, ((0, 2), (1, 128))),
        "audio_query": centred(key_of[6], (2, AUD_TOKENS, HW), 1.0, 6.0, ((0, 2), (1, 128))),
        "audio_self_query": centred(key_of[7], (2, AUD_TOKENS, HW), 1.0, 6.0, ((0, 2), (1, 128))),
        "audio_self_key": centred(key_of[8], (2, AUD_TOKENS, HW), 1.0, 6.0, ((0, 2), (1, 128))),
        "audio_self_value": centred(key_of[9], (2, AUD_TOKENS, HW), 1.0, 6.0, ((0, 2), (1, 128))),
        "v2a_qgain": jnp.clip(1.0 + 0.18 * jax.random.normal(key_of[10], (HW,), jnp.float32), 0.1, 1.9),
        "v2a_kgain": jnp.clip(1.0 + 0.18 * jax.random.normal(key_of[11], (HW,), jnp.float32), 0.1, 1.9),
        "self_qgain": jnp.clip(1.0 + 0.18 * jax.random.normal(key_of[12], (HW,), jnp.float32), 0.1, 1.9),
        "self_kgain": jnp.clip(1.0 + 0.18 * jax.random.normal(key_of[13], (HW,), jnp.float32), 0.1, 1.9),
        "a2v_qgain": jnp.clip(1.0 + 0.18 * jax.random.normal(key_of[14], (HW,), jnp.float32), 0.1, 1.9),
        "a2v_kgain": jnp.clip(1.0 + 0.18 * jax.random.normal(key_of[15], (HW,), jnp.float32), 0.1, 1.9),
        "video_time": with_ends(jax.random.randint(key_of[16], (VID_TOKENS,), 0, 2048), jax.random.fold_in(key_of[16], 1), 0, 2047).astype(jnp.int32),
        "audio_time": with_ends(jax.random.randint(key_of[17], (AUD_TOKENS,), 0, 2048), jax.random.fold_in(key_of[17], 1), 0, 2047).astype(jnp.int32),
        "branch_keep": draw_branch_keep(jax.random.fold_in(key_of[19], 71), 0),
    }


epsilon = 1e-06
rope_base = 10000.0
guide_scale = 3.0

def rotate_norm(tensor, gain_vec, positions):
    row_count = tensor.shape[0]
    by_head = tensor.astype(jnp.float32).reshape(row_count, HEADS, HEAD_DIM)
    scaled = by_head * lax.rsqrt(lax.optimization_barrier(jnp.mean(by_head * by_head, axis=-1, keepdims=True)) + epsilon)
    scaled = scaled * gain_vec.reshape(HEADS, HEAD_DIM)
    half_dim = HEAD_DIM // 2
    frequencies = rope_base ** (-jnp.arange(half_dim, dtype=jnp.float32) / half_dim)
    angles = positions.astype(jnp.float32)[:, None] * frequencies[None, :]
    cos_table = jnp.cos(angles)[:, None, :]
    sin_table = jnp.sin(angles)[:, None, :]
    lower_half = scaled[..., :half_dim]
    upper_half = scaled[..., half_dim:]
    turned = jnp.concatenate([lower_half * cos_table - upper_half * sin_table, upper_half * cos_table + lower_half * sin_table], axis=-1)
    return turned.reshape(row_count, HEADS * HEAD_DIM).astype(jnp.bfloat16)

def split_heads(tensor):
    return tensor.reshape(tensor.shape[0], HEADS, HEAD_DIM).transpose(1, 0, 2)

def attend(query_rows, key_rows, value_rows, key_weight):
    row_count = query_rows.shape[0]

    def one_head(head_items):
        head_query, head_key, head_value = head_items
        scores = jnp.dot(head_query, head_key.T, preferred_element_type=jnp.float32) / math.sqrt(HEAD_DIM)
        weights = jnp.exp(scores) * key_weight[None, :]
        totals = lax.optimization_barrier(jnp.sum(weights, axis=1, keepdims=True))
        numerator = jnp.dot(weights.astype(jnp.bfloat16), head_value, preferred_element_type=jnp.float32)
        return numerator / totals
    result = lax.map(one_head, (split_heads(query_rows), split_heads(key_rows), split_heads(value_rows)))
    return result.transpose(1, 0, 2).reshape(row_count, HEADS * HEAD_DIM)

def combine_branches(cond_part, uncond_part):
    uncond_f = uncond_part.astype(jnp.float32)
    return (uncond_f + guide_scale * (cond_part.astype(jnp.float32) - uncond_f)).astype(jnp.bfloat16)

def reference(video_hidden, video_weight, video_key, video_value, audio_cross_key, audio_cross_value, audio_query, audio_self_query, audio_self_key, audio_self_value, v2a_qgain, v2a_kgain, self_qgain, self_kgain, a2v_qgain, a2v_kgain, video_time, audio_time, branch_keep):
    video_parts = []
    audio_parts = []
    for branch in range(2):
        projected = jnp.dot(video_hidden[branch], video_weight, preferred_element_type=jnp.float32)
        video_queries = rotate_norm(projected, v2a_qgain, video_time)
        cross_keys = rotate_norm(audio_cross_key[branch], v2a_kgain, audio_time)
        self_queries = rotate_norm(audio_self_query[branch], self_qgain, audio_time)
        self_keys = rotate_norm(audio_self_key[branch], self_kgain, audio_time)
        audio_queries = rotate_norm(audio_query[branch], a2v_qgain, audio_time)
        video_keys = rotate_norm(video_key[branch], a2v_kgain, video_time)
        kept_keys = branch_keep[branch].astype(jnp.float32)
        video_part = attend(video_queries, cross_keys, audio_cross_value[branch], kept_keys).astype(jnp.bfloat16)
        self_part = attend(self_queries, self_keys, audio_self_value[branch], kept_keys)
        all_video = jnp.ones((video_keys.shape[0],), jnp.float32)
        cross_part = attend(audio_queries, video_keys, video_value[branch], all_video)
        video_parts.append(video_part)
        audio_parts.append((self_part + cross_part).astype(jnp.bfloat16))
    video_guided = combine_branches(video_parts[0], video_parts[1])
    audio_guided = combine_branches(audio_parts[0], audio_parts[1])
    return (video_guided, audio_guided)
```

```python
import math

import jax
import jax.numpy as jnp
from jax import lax
from jax.experimental import pallas as pl
from jax.experimental.pallas import tpu as pltpu
from jax.sharding import PartitionSpec as P

HEADS = 12
HEAD_DIM = 128
MESH = pl.DeviceIdType.MESH

epsilon = 1e-06
rope_base = 10000.0
guide_scale = 3.0

GROUP = 3
GW = GROUP * HEAD_DIM
CK, CV, KEEP, SK, SV, AQ = 0, 384, 768, 896, 1280, 1664
SIBLING_LANES = 1664
BLOCK_LANES = 2048
SCORE_SCALE = math.log2(math.e) / math.sqrt(HEAD_DIM)
NT = (((1,), (1,)), ((), ()))


def rope_head(rows, gain, cos, sin):
    mean = jnp.mean(rows * rows, axis=1, keepdims=True)
    scaled = rows * lax.rsqrt(mean + epsilon) * gain
    return scaled * cos + pltpu.roll(scaled, 64, 1) * sin


def weigh(queries, keys, values):
    scores = lax.dot_general(queries, keys, NT, preferred_element_type=jnp.float32)
    weights = jnp.exp2(scores * SCORE_SCALE).astype(jnp.bfloat16)
    return jnp.dot(weights, values, preferred_element_type=jnp.float32)


def head(index):
    return slice(index * HEAD_DIM, (index + 1) * HEAD_DIM)


def kernel(
    hidden,
    weight,
    video_key,
    video_value,
    cross_key,
    cross_value,
    audio_query,
    self_query,
    self_key,
    self_value,
    v2a_qgain,
    v2a_kgain,
    self_qgain,
    self_kgain,
    a2v_qgain,
    a2v_kgain,
    video_cos,
    video_sin,
    audio_cos,
    audio_sin,
    keep,
    video_out,
    audio_out,
    wbuf,
    astage,
    arcv,
    block,
    squery,
    vq_send,
    vk_send,
    vq,
    vk,
    vv,
    partial,
    partials,
    vpart,
    apart,
    vfin,
    afin,
    w_sem,
    za_s,
    za_r,
    zk_s,
    zk_r,
    zv_s,
    zv_r,
    zq_s,
    zq_r,
    x_s,
    x_r,
    y_s,
    y_r,
    fa_s,
    fa_r,
    fb_s,
    fb_r,
    sib_s,
    sib_r,
    sibv_s,
    sibv_r,
    rs_s,
    rs_r,
    vf_s,
    vf_r,
    af_s,
    af_r,
):
    cfg = lax.axis_index("cfg")
    seq = lax.axis_index("seq")
    core = lax.rem(seq, 2)
    y = lax.rem(seq // 2, 4)
    zh = lax.rem(seq // 8, 4)
    x = seq // 32

    def device(cfg_, x_, zh_, y_, core_):
        return (cfg_, ((x_ * 4 + zh_) * 4 + y_) * 2 + core_)

    def plus(value, d):
        return lax.rem(value + d, 4)

    def minus(value, d):
        return lax.rem(value + 4 - d, 4)

    sibling = device(cfg, x, zh, y, 1 - core)

    def remote(src, dst, send, recv, target):
        return pltpu.make_async_remote_copy(
            src_ref=src,
            dst_ref=dst,
            send_sem=send,
            recv_sem=recv,
            device_id=target,
            device_id_type=MESH,
        )

    sends = []

    def start(*args):
        copy = remote(*args)
        copy.start()
        sends.append(copy)

    def arrived(dst, send, recv):
        remote(dst, dst, send, recv, sibling).wait_recv()

    weight_copies = [
        pltpu.make_async_copy(
            weight.at[:, pl.ds(n * 256, 256)], wbuf.at[n], w_sem.at[n]
        )
        for n in range(6)
    ]
    for copy in weight_copies:
        copy.start()

    barrier = pltpu.get_barrier_semaphore()
    peers = [sibling]
    for dx in range(4):
        for dy in range(4):
            if dx or dy:
                peers.append(device(cfg, plus(x, dx), zh, plus(y, dy), core))
    for d in range(4):
        if d:
            peers.append(device(cfg, x, plus(zh, d), y, core))
        peers.append(device(1 - cfg, x, plus(zh, d), y, core))
    for peer in peers:
        pl.semaphore_signal(barrier, inc=1, device_id=peer, device_id_type=MESH)

    acos, asin = audio_cos[...], audio_sin[...]
    mask = keep[...]
    nothing = jnp.zeros((8, HEAD_DIM), jnp.float32)
    for h in range(HEADS):
        at = head(h)

        def rows(ref):
            return ref[0, :, at].astype(jnp.float32)

        pieces = [
            rope_head(rows(audio_query), a2v_qgain[:, at], acos, asin),
            rope_head(rows(self_query), self_qgain[:, at], acos, asin),
            rope_head(rows(cross_key), v2a_kgain[:, at], acos, asin),
            rows(cross_value) * mask,
            rope_head(rows(self_key), self_kgain[:, at], acos, asin),
            rows(self_value) * mask,
            mask,
            nothing,
        ]
        astage[h // GROUP, :, head(h % GROUP)] = jnp.concatenate(pieces, axis=0).astype(
            jnp.bfloat16
        )

    pl.semaphore_wait(barrier, len(peers))

    for d in (1, 3, 2):
        to = plus(zh, d)
        start(
            astage.at[to],
            arcv.at[zh],
            za_s.at[d - 1],
            za_r.at[d - 1],
            device(cfg, x, to, y, core),
        )
    arcv[zh] = astage[zh]

    own_half = pl.multiple_of(core * 256, 256)
    own_rows = pl.multiple_of(core * 256 + zh * 64, 64)
    own_lanes = pl.multiple_of(zh * GW, 128)
    for d in (1, 3, 2):
        to = plus(zh, d)
        start(
            video_value.at[0, :, pl.ds(pl.multiple_of(to * GW, 128), GW)],
            vv.at[pl.ds(own_rows, 64)],
            zv_s.at[d - 1],
            zv_r.at[d - 1],
            device(cfg, x, to, y, core),
        )
    vv[pl.ds(own_rows, 64)] = video_value[0, :, pl.ds(own_lanes, GW)]
    vcos, vsin = video_cos[...], video_sin[...]
    for h in range(HEADS):
        at = head(h)
        vk_send[:, at] = rope_head(
            video_key[0, :, at].astype(jnp.float32), a2v_kgain[:, at], vcos, vsin
        ).astype(jnp.bfloat16)
    for d in (1, 3, 2):
        to = plus(zh, d)
        start(
            vk_send.at[:, pl.ds(pl.multiple_of(to * GW, 128), GW)],
            vk.at[pl.ds(own_rows, 64)],
            zk_s.at[d - 1],
            zk_r.at[d - 1],
            device(cfg, x, to, y, core),
        )
    vk[pl.ds(own_rows, 64)] = vk_send[:, pl.ds(own_lanes, GW)]

    for d in (1, 3, 2):
        arrived(arcv.at[minus(zh, d)], za_s.at[d - 1], za_r.at[d - 1])
    received = [arcv[z].astype(jnp.float32) for z in range(4)]

    def kind(k):
        return jnp.concatenate(
            [one[8 * k : 8 * k + 8] for one in received], axis=0
        ).astype(jnp.bfloat16)

    def base_of(core_, x_, y_):
        return pl.multiple_of(core_ * 512 + (x_ * 4 + y_) * 32, 32)

    own_block = base_of(core, x, y)
    squery[...] = kind(1)
    for k, lane in ((0, AQ), (2, CK), (3, CV), (4, SK), (5, SV)):
        block[pl.ds(own_block, 32), lane : lane + GW] = kind(k)
    block[pl.ds(own_block, 32), KEEP : KEEP + HEAD_DIM] = kind(6)[:, :HEAD_DIM]

    def whole(x_, y_):
        return block.at[pl.ds(base_of(core, x_, y_), 32)]

    def half(x_, y_, which):
        return block.at[pl.ds(pl.multiple_of(base_of(core, x_, y_) + 16 * which, 16), 16)]

    def shared(core_, x_, y_):
        return block.at[pl.ds(base_of(core_, x_, y_), 32), pl.ds(0, SIBLING_LANES)]

    def shared_half(core_, x_, y_, which):
        return block.at[
            pl.ds(pl.multiple_of(base_of(core_, x_, y_) + 16 * which, 16), 16),
            pl.ds(0, SIBLING_LANES),
        ]

    for d in (1, 3, 2):
        start(
            whole(x, y),
            whole(x, y),
            x_s.at[d - 1],
            x_r.at[d - 1],
            device(cfg, plus(x, d), zh, y, core),
        )
        start(
            whole(x, y),
            whole(x, y),
            y_s.at[d - 1],
            y_r.at[d - 1],
            device(cfg, x, zh, plus(y, d), core),
        )
    start(shared(core, x, y), shared(core, x, y), sib_s.at[0], sib_r.at[0], sibling)

    def project(n):
        weight_copies[n].wait()
        product = jnp.dot(hidden[0], wbuf[n], preferred_element_type=jnp.float32)
        for part in range(2):
            at = head(2 * n + part)
            vq_send[:, at] = rope_head(
                product[:, head(part)], v2a_qgain[:, at], vcos, vsin
            ).astype(jnp.bfloat16)

    for n in range(3):
        project(n)

    for d1 in (1, 3, 2):
        sx, sy = minus(x, d1), minus(y, d1)
        arrived(whole(sx, y), x_s.at[d1 - 1], x_r.at[d1 - 1])
        for d2 in (1, 3, 2):
            slot = (d1 - 1) * 3 + d2 - 1
            start(
                half(sx, y, 0),
                half(sx, y, 0),
                fa_s.at[slot],
                fa_r.at[slot],
                device(cfg, x, zh, plus(y, d2), core),
            )
        start(
            shared(core, sx, y), shared(core, sx, y), sib_s.at[d1], sib_r.at[d1], sibling
        )
        arrived(whole(x, sy), y_s.at[d1 - 1], y_r.at[d1 - 1])
        for d2 in (1, 3, 2):
            slot = (d1 - 1) * 3 + d2 - 1
            start(
                half(x, sy, 1),
                half(x, sy, 1),
                fb_s.at[slot],
                fb_r.at[slot],
                device(cfg, plus(x, d2), zh, y, core),
            )
        start(
            shared(core, x, sy),
            shared(core, x, sy),
            sib_s.at[3 + d1],
            sib_r.at[3 + d1],
            sibling,
        )

    for d in (1, 3, 2):
        there = pl.multiple_of(core * 256 + minus(zh, d) * 64, 64)
        arrived(vv.at[pl.ds(there, 64)], zv_s.at[d - 1], zv_r.at[d - 1])
        arrived(vk.at[pl.ds(there, 64)], zk_s.at[d - 1], zk_r.at[d - 1])
    mine = pl.ds(own_half, 256)
    start(vv.at[mine], vv.at[mine], sibv_s.at[0], sibv_r.at[0], sibling)
    start(vk.at[mine], vk.at[mine], sibv_s.at[1], sibv_r.at[1], sibling)

    for n in range(3, 6):
        project(n)
    for d in (1, 3, 2):
        to = plus(zh, d)
        start(
            vq_send.at[:, pl.ds(pl.multiple_of(to * GW, 128), GW)],
            vq.at[pl.ds(pl.multiple_of(zh * 64, 64), 64)],
            zq_s.at[d - 1],
            zq_r.at[d - 1],
            device(cfg, x, to, y, core),
        )
    vq[pl.ds(pl.multiple_of(zh * 64, 64), 64)] = vq_send[:, pl.ds(own_lanes, GW)]

    for d1 in (1, 3, 2):
        for d2 in (1, 3, 2):
            slot = (d1 - 1) * 3 + d2 - 1
            sx, sy = minus(x, d1), minus(y, d2)
            arrived(half(sx, sy, 0), fa_s.at[slot], fa_r.at[slot])
            piece = shared_half(core, sx, sy, 0)
            start(piece, piece, sib_s.at[7 + slot], sib_r.at[7 + slot], sibling)
            sx, sy = minus(x, d2), minus(y, d1)
            arrived(half(sx, sy, 1), fb_s.at[slot], fb_r.at[slot])
            piece = shared_half(core, sx, sy, 1)
            start(piece, piece, sib_s.at[16 + slot], sib_r.at[16 + slot], sibling)

    other = 1 - core
    other_half = pl.ds(pl.multiple_of(other * 256, 256), 256)
    arrived(vv.at[other_half], sibv_s.at[0], sibv_r.at[0])
    arrived(vk.at[other_half], sibv_s.at[1], sibv_r.at[1])
    ones = jnp.ones((512, HEAD_DIM), jnp.bfloat16)
    lane = lax.broadcasted_iota(jnp.int32, (128, HEAD_DIM), 1)
    for dx in (1, 3, 2, 0):
        px = plus(x, dx)
        row = pl.multiple_of(px * 128, 128)
        packed = jnp.zeros((128, HEAD_DIM), jnp.float32)
        for h in range(GROUP):
            queries = block[
                pl.ds(pl.multiple_of(core * 512 + row, 128), 128),
                AQ + h * HEAD_DIM : AQ + (h + 1) * HEAD_DIM,
            ]
            values = jnp.concatenate([vv[:, head(h)], ones], axis=1)
            both = weigh(queries, vk[:, head(h)], values)
            partial[pl.ds(row, 128), head(h)] = both[:, :HEAD_DIM].astype(jnp.bfloat16)
            total = both[:, HEAD_DIM:]
            high = total.astype(jnp.bfloat16).astype(jnp.float32)
            packed = jnp.where(lane // 16 == 2 * h, high, packed)
            packed = jnp.where(lane // 16 == 2 * h + 1, total - high, packed)
        partial[pl.ds(row, 128), GW : GW + HEAD_DIM] = packed.astype(jnp.bfloat16)
        for dy in (1, 3, 2, 0):
            if dx or dy:
                py = plus(y, dy)
                start(
                    partial.at[pl.ds(pl.multiple_of((px * 4 + py) * 32, 32), 32)],
                    partials.at[x * 4 + y],
                    rs_s.at[dx * 4 + dy],
                    rs_r.at[dx * 4 + dy],
                    device(cfg, px, zh, py, core),
                )
    partials[x * 4 + y] = partial[pl.ds(pl.multiple_of((x * 4 + y) * 32, 32), 32)]

    arrived(shared(other, x, y), sib_s.at[0], sib_r.at[0])
    for d1 in (1, 3, 2):
        arrived(shared(other, minus(x, d1), y), sib_s.at[d1], sib_r.at[d1])
        arrived(shared(other, x, minus(y, d1)), sib_s.at[3 + d1], sib_r.at[3 + d1])
    for d1 in (1, 3, 2):
        for d2 in (1, 3, 2):
            slot = (d1 - 1) * 3 + d2 - 1
            arrived(
                shared_half(other, minus(x, d1), minus(y, d2), 0),
                sib_s.at[7 + slot],
                sib_r.at[7 + slot],
            )
            arrived(
                shared_half(other, minus(x, d2), minus(y, d1), 1),
                sib_s.at[16 + slot],
                sib_r.at[16 + slot],
            )
    for d in (1, 3, 2):
        arrived(
            vq.at[pl.ds(pl.multiple_of(minus(zh, d) * 64, 64), 64)],
            zq_s.at[d - 1],
            zq_r.at[d - 1],
        )

    is_final = cfg == zh // 2
    slot_out = cfg * 2 + lax.rem(zh, 2)
    final_cfg = zh // 2
    near_copies = []
    for d in (1, 3, 2, 0):
        z = plus(zh, d)
        row = pl.multiple_of(z * 64, 64)
        for h in range(GROUP):
            values = jnp.concatenate(
                [block[:, CV + h * HEAD_DIM : CV + (h + 1) * HEAD_DIM], block[:, KEEP:SK]],
                axis=1,
            )
            both = weigh(
                vq[pl.ds(row, 64), head(h)],
                block[:, CK + h * HEAD_DIM : CK + (h + 1) * HEAD_DIM],
                values,
            )
            vpart[pl.ds(row, 64), head(h)] = (
                both[:, :HEAD_DIM] / both[:, HEAD_DIM:]
            ).astype(jnp.bfloat16)
        copy = remote(
            vpart.at[pl.ds(row, 64)],
            vfin.at[slot_out],
            vf_s.at[d],
            vf_r.at[slot_out],
            device(final_cfg, x, z, y, core),
        )
        if d:
            copy.start()
            sends.append(copy)
        else:
            pl.when(jnp.logical_not(is_final))(copy.start)
            near_copies.append(copy)

    for h in range(GROUP):
        values = jnp.concatenate(
            [block[:, SV + h * HEAD_DIM : SV + (h + 1) * HEAD_DIM], block[:, KEEP:SK]],
            axis=1,
        )
        both = weigh(
            squery[:, head(h)],
            block[:, SK + h * HEAD_DIM : SK + (h + 1) * HEAD_DIM],
            values,
        )
        apart[:, head(h)] = both[:, :HEAD_DIM] / both[:, HEAD_DIM:]

    for dx in (1, 3, 2, 0):
        for dy in (1, 3, 2, 0):
            if dx or dy:
                arrived(
                    partials.at[minus(x, dx) * 4 + minus(y, dy)],
                    rs_s.at[dx * 4 + dy],
                    rs_r.at[dx * 4 + dy],
                )
    summed = partials[0].astype(jnp.float32)
    for n in range(1, 16):
        summed = summed + partials[n].astype(jnp.float32)
    for h in range(GROUP):
        high = summed[:, GW + 32 * h : GW + 32 * h + 1]
        low = summed[:, GW + 32 * h + 16 : GW + 32 * h + 17]
        part = apart[:, head(h)] + summed[:, head(h)] / (high + low)
        apart[:, head(h)] = part.astype(jnp.bfloat16).astype(jnp.float32)
    for d in (1, 3, 2, 0):
        z = plus(zh, d)
        copy = remote(
            apart.at[pl.ds(pl.multiple_of(z * 8, 8), 8)],
            afin.at[slot_out],
            af_s.at[d],
            af_r.at[slot_out],
            device(final_cfg, x, z, y, core),
        )
        if d:
            copy.start()
            sends.append(copy)
        else:
            pl.when(jnp.logical_not(is_final))(copy.start)
            near_copies.append(copy)

    @pl.when(is_final)
    def _():
        vfin[slot_out] = vpart[pl.ds(pl.multiple_of(zh * 64, 64), 64)]
        afin[slot_out] = apart[pl.ds(pl.multiple_of(zh * 8, 8), 8)]

    def wait_final(fin, send, recv):
        for b in range(2):
            for j in range(2):
                here = jnp.logical_and(cfg == b, zh == 2 * cfg + j)

                @pl.when(jnp.logical_not(here))
                def _():
                    arrived(fin.at[2 * b + j], send.at[0], recv.at[2 * b + j])

    def guide(cond, uncond):
        uncond = uncond.astype(jnp.float32)
        return (uncond + guide_scale * (cond.astype(jnp.float32) - uncond)).astype(
            jnp.bfloat16
        )

    wait_final(vfin, vf_s, vf_r)
    for j in range(2):
        video_out[:, j * GW : (j + 1) * GW] = guide(vfin[j], vfin[2 + j])
    wait_final(afin, af_s, af_r)
    audio_out[...] = jnp.concatenate([guide(afin[j], afin[2 + j]) for j in range(2)], axis=1)

    for copy in sends:
        copy.wait_send()

    @pl.when(jnp.logical_not(is_final))
    def _():
        for copy in near_copies:
            copy.wait_send()


def per_device(
    video_hidden,
    video_weight,
    video_key,
    video_value,
    audio_cross_key,
    audio_cross_value,
    audio_query,
    audio_self_query,
    audio_self_key,
    audio_self_value,
    v2a_qgain,
    v2a_kgain,
    self_qgain,
    self_kgain,
    a2v_qgain,
    a2v_kgain,
    video_time,
    audio_time,
    branch_keep,
):
    half_dim = HEAD_DIM // 2
    frequencies = rope_base ** (-jnp.arange(half_dim, dtype=jnp.float32) / half_dim)
    frequencies = jnp.concatenate([frequencies, frequencies])
    turn = jnp.where(jnp.arange(HEAD_DIM) < half_dim, -1.0, 1.0).astype(jnp.float32)

    def tables(positions):
        angles = positions.astype(jnp.float32)[:, None] * frequencies[None, :]
        return jnp.cos(angles), jnp.sin(angles) * turn

    video_cos, video_sin = tables(video_time)
    audio_cos, audio_sin = tables(audio_time)
    keep = jnp.broadcast_to(branch_keep[0].astype(jnp.float32)[:, None], (8, HEAD_DIM))

    vmem = pl.BlockSpec(memory_space=pltpu.VMEM)
    bf16, f32 = jnp.bfloat16, jnp.float32
    dma = pltpu.SemaphoreType.DMA
    gains = [
        gain.reshape(1, HEADS * HEAD_DIM)
        for gain in (v2a_qgain, v2a_kgain, self_qgain, self_kgain, a2v_qgain, a2v_kgain)
    ]
    return pl.pallas_call(
        kernel,
        out_shape=(
            jax.ShapeDtypeStruct((64, 2 * GW), bf16),
            jax.ShapeDtypeStruct((8, 2 * GW), bf16),
        ),
        in_specs=[vmem, pl.BlockSpec(memory_space=pl.ANY)] + [vmem] * 19,
        out_specs=(vmem, vmem),
        scratch_shapes=[
            pltpu.VMEM((6, 3072, 256), bf16),
            pltpu.VMEM((4, 64, GW), bf16),
            pltpu.VMEM((4, 64, GW), bf16),
            pltpu.VMEM((1024, BLOCK_LANES), bf16),
            pltpu.VMEM((32, GW), bf16),
            pltpu.VMEM((64, 4 * GW), bf16),
            pltpu.VMEM((64, 4 * GW), bf16),
            pltpu.VMEM((256, GW), bf16),
            pltpu.VMEM((512, GW), bf16),
            pltpu.VMEM((512, GW), bf16),
            pltpu.VMEM((512, 512), bf16),
            pltpu.VMEM((16, 32, 512), bf16),
            pltpu.VMEM((256, GW), bf16),
            pltpu.VMEM((32, GW), f32),
            pltpu.VMEM((4, 64, GW), bf16),
            pltpu.VMEM((4, 8, GW), f32),
            dma((6,)),
            dma((3,)),
            dma((3,)),
            dma((3,)),
            dma((3,)),
            dma((3,)),
            dma((3,)),
            dma((3,)),
            dma((3,)),
            dma((3,)),
            dma((3,)),
            dma((3,)),
            dma((3,)),
            dma((9,)),
            dma((9,)),
            dma((9,)),
            dma((9,)),
            dma((25,)),
            dma((25,)),
            dma((2,)),
            dma((2,)),
            dma((16,)),
            dma((16,)),
            dma((4,)),
            dma((4,)),
            dma((4,)),
            dma((4,)),
        ],
        compiler_params=pltpu.CompilerParams(
            collective_id=0, has_side_effects=True, vmem_limit_bytes=48 * 1024 * 1024
        ),
        cost_estimate=pl.CostEstimate(
            flops=2 * 64 * 3072 * 1536 * 3, bytes_accessed=12_000_000, transcendentals=1_700_000
        ),
    )(
        video_hidden,
        video_weight,
        video_key,
        video_value,
        audio_cross_key,
        audio_cross_value,
        audio_query,
        audio_self_query,
        audio_self_key,
        audio_self_value,
        *gains,
        video_cos,
        video_sin,
        audio_cos,
        audio_sin,
        keep,
    )


def solution(mesh):
    in_specs = (
        P("cfg", "seq", None),
        P(),
        P("cfg", "seq", None),
        P("cfg", "seq", None),
        P("cfg", "seq", None),
        P("cfg", "seq", None),
        P("cfg", "seq", None),
        P("cfg", "seq", None),
        P("cfg", "seq", None),
        P("cfg", "seq", None),
        P(),
        P(),
        P(),
        P(),
        P(),
        P(),
        P("seq"),
        P("seq"),
        P("cfg", "seq"),
    )
    out_specs = (P("seq", "cfg"), P("seq", "cfg"))
    return jax.shard_map(
        per_device, mesh=mesh, in_specs=in_specs, out_specs=out_specs, check_vma=False
    )
```

```python
import math

import jax
import jax.numpy as jnp
import numpy as np
from jax import lax
from jax.experimental import pallas as pl
from jax.experimental.pallas import tpu as pltpu
from jax.sharding import PartitionSpec as P

HEADS = 12
HEAD_DIM = 128
MESH = pl.DeviceIdType.MESH

epsilon = 1e-06
rope_base = 10000.0
guide_scale = 3.0

GROUP = 3
GW = GROUP * HEAD_DIM
CK, CV, KEEP, KV_LANES = 0, 384, 768, 896
SUM_LANES = GW + HEAD_DIM
SCORE_SCALE = math.log2(math.e) / math.sqrt(HEAD_DIM)
NT = (((1,), (1,)), ((), ()))


def rope_heads(items):
    means = [jnp.mean(rows * rows, axis=1, keepdims=True) for rows, _, _, _ in items]
    scaled = [
        rows * lax.rsqrt(mean + epsilon) * gain
        for mean, (rows, gain, _, _) in zip(means, items)
    ]
    turned = [pltpu.roll(one, 64, 1) for one in scaled]
    return [
        one * cos + other * sin
        for one, other, (_, _, cos, sin) in zip(scaled, turned, items)
    ]


def weigh(queries, keys, values):
    scores = lax.dot_general(queries, keys, NT, preferred_element_type=jnp.float32)
    weights = jnp.exp2(scores * SCORE_SCALE).astype(jnp.bfloat16)
    return jnp.dot(weights, values, preferred_element_type=jnp.float32)


def head(index, base=0):
    return slice(base + index * HEAD_DIM, base + (index + 1) * HEAD_DIM)


TRANSFERS = (
    ("z1", 3),
    ("z2", 3),
    ("zk", 3),
    ("zv", 3),
    ("zq", 3),
    ("g0ax", 3),
    ("g0by", 3),
    ("g0ay", 3),
    ("g0bx", 3),
    ("g1ax", 3),
    ("g1by", 3),
    ("g1ay", 3),
    ("g1bx", 3),
    ("sqx", 3),
    ("sky", 3),
    ("sib", 4),
    ("rs", 16),
    ("ss", 3),
    ("vf", 4),
    ("af", 4),
)
FIRST = {}
for _name, _count in TRANSFERS:
    FIRST[_name] = sum(c for n, c in TRANSFERS if n in FIRST)
SEMAPHORES = sum(c for _, c in TRANSFERS)


def kernel(
    hidden_hbm,
    weight,
    video_key_hbm,
    video_value,
    cross_key_hbm,
    cross_value_hbm,
    audio_query_hbm,
    self_query_hbm,
    self_key_hbm,
    self_value_hbm,
    v2a_qgain_hbm,
    v2a_kgain_hbm,
    self_qgain_hbm,
    self_kgain_hbm,
    a2v_qgain_hbm,
    a2v_kgain_hbm,
    video_time,
    audio_time,
    branch_keep,
    frequency,
    vfin,
    afin,
    hidden_in,
    key_in,
    audio_in,
    gain_in,
    frequency_in,
    video_clock,
    audio_clock,
    keep_in,
    in_sem,
    wbuf,
    w_sem,
    stage1,
    stage2,
    recv1,
    recv2,
    g0,
    g1,
    squery,
    sblock,
    spartial,
    spartials,
    vq_send,
    vk_send,
    vq,
    vk,
    vv,
    partial,
    partials,
    vpart,
    apart,
    send_sem,
    recv_sem,
):
    cfg = lax.axis_index("cfg")
    seq = lax.axis_index("seq")
    core = lax.rem(seq, 2)
    y = lax.rem(seq // 2, 4)
    zh = lax.rem(seq // 8, 4)
    x = seq // 32
    other = 1 - core
    me = core

    def device(cfg_, x_, zh_, y_, core_):
        return (cfg_, ((x_ * 4 + zh_) * 4 + y_) * 2 + core_)

    def plus(value, d):
        return lax.rem(value + d, 4)

    def minus(value, d):
        return lax.rem(value + 4 - d, 4)

    def aligned(value, to):
        return pl.multiple_of(value, to)

    sibling = device(cfg, x, zh, y, other)

    def remote(src, dst, send, recv, target):
        return pltpu.make_async_remote_copy(
            src_ref=src,
            dst_ref=dst,
            send_sem=send_sem.at[send],
            recv_sem=recv_sem.at[recv],
            device_id=target,
            device_id_type=MESH,
        )

    sends = []

    def start(src, dst, name, index, target):
        copy = remote(src, dst, FIRST[name] + index, FIRST[name] + index, target)
        copy.start()
        sends.append(copy)

    def arrived(dst, name, index):
        remote(dst, dst, FIRST[name], FIRST[name] + index, sibling).wait_recv()

    inputs = [
        (audio_time, audio_clock),
        (branch_keep.at[0], keep_in),
        (frequency, frequency_in),
        (audio_query_hbm.at[0], audio_in.at[0]),
        (cross_key_hbm.at[0], audio_in.at[2]),
        (cross_value_hbm.at[0], audio_in.at[3]),
        (a2v_qgain_hbm, gain_in.at[0]),
        (v2a_kgain_hbm, gain_in.at[2]),
        (self_query_hbm.at[0], audio_in.at[1]),
        (self_key_hbm.at[0], audio_in.at[4]),
        (self_value_hbm.at[0], audio_in.at[5]),
        (self_qgain_hbm, gain_in.at[1]),
        (self_kgain_hbm, gain_in.at[3]),
        (video_time, video_clock),
        (video_key_hbm.at[0], key_in),
        (a2v_kgain_hbm, gain_in.at[4]),
        (v2a_qgain_hbm, gain_in.at[5]),
        (hidden_hbm.at[0], hidden_in),
    ]
    input_copies = [
        pltpu.make_async_copy(src, dst, in_sem.at[n])
        for n, (src, dst) in enumerate(inputs)
    ]
    for copy in input_copies:
        copy.start()

    barrier = pltpu.get_barrier_semaphore()
    peers = [sibling]
    for dx in range(4):
        for dy in range(4):
            if dx or dy:
                peers.append(device(cfg, plus(x, dx), zh, plus(y, dy), core))
    for d in range(4):
        if d:
            peers.append(device(cfg, x, plus(zh, d), y, core))
        peers.append(device(1 - cfg, x, plus(zh, d), y, core))
    for peer in peers:
        pl.semaphore_signal(barrier, inc=1, device_id=peer, device_id_type=MESH)

    weight_copies = [
        pltpu.make_async_copy(
            weight.at[:, pl.ds(n * 256, 256)], wbuf.at[n], w_sem.at[n]
        )
        for n in range(6)
    ]
    for copy in weight_copies:
        copy.start()

    def spread(scalars, count):
        row = lax.broadcasted_iota(jnp.int32, (8, HEAD_DIM), 0)
        tiles = []
        for first in range(0, count, 8):
            tile = jnp.zeros((8, HEAD_DIM), jnp.int32)
            for r in range(8):
                tile = jnp.where(row == r, scalars[first + r], tile)
            tiles.append(tile)
        return jnp.concatenate(tiles, axis=0).astype(jnp.float32)

    def tables(scalars, count):
        angles = spread(scalars, count) * frequency_in[...]
        lanes = lax.broadcasted_iota(jnp.int32, (count, HEAD_DIM), 1)
        sin = jnp.sin(angles)
        return jnp.cos(angles), jnp.where(lanes < HEAD_DIM // 2, -sin, sin)

    def gain(which, h):
        return gain_in[which, head(h)].reshape(1, HEAD_DIM)

    def audio_rows(which, h):
        return audio_in[which, :, head(h)].astype(jnp.float32)

    for copy in input_copies[:8]:
        copy.wait()
    acos, asin = tables(audio_clock, 8)
    mask = spread(keep_in, 8)
    nothing = jnp.zeros((8, HEAD_DIM), jnp.float32)
    ropes = rope_heads(
        [(audio_rows(0, h), gain(0, h), acos, asin) for h in range(HEADS)]
        + [(audio_rows(2, h), gain(2, h), acos, asin) for h in range(HEADS)]
    )
    values = [audio_rows(3, h) * mask for h in range(HEADS)]
    for h in range(HEADS):
        pieces = [ropes[h], ropes[HEADS + h], values[h], mask]
        stage1[h // GROUP, :, head(h % GROUP)] = jnp.concatenate(pieces, axis=0).astype(
            jnp.bfloat16
        )

    pl.semaphore_wait(barrier, len(peers))

    for d in (1, 3, 2):
        to = plus(zh, d)
        start(stage1.at[to], recv1.at[zh], "z1", d - 1, device(cfg, x, to, y, core))
    recv1[zh] = stage1[zh]

    for copy in input_copies[8:13]:
        copy.wait()
    ropes = rope_heads(
        [(audio_rows(1, h), gain(1, h), acos, asin) for h in range(HEADS)]
        + [(audio_rows(4, h), gain(3, h), acos, asin) for h in range(HEADS)]
    )
    values = [audio_rows(5, h) * mask for h in range(HEADS)]
    for h in range(HEADS):
        pieces = [ropes[h], ropes[HEADS + h], values[h], nothing]
        stage2[h // GROUP, :, head(h % GROUP)] = jnp.concatenate(pieces, axis=0).astype(
            jnp.bfloat16
        )
    for d in (1, 3, 2):
        to = plus(zh, d)
        start(stage2.at[to], recv2.at[zh], "z2", d - 1, device(cfg, x, to, y, core))
    recv2[zh] = stage2[zh]

    for copy in input_copies[13:16]:
        copy.wait()
    vcos, vsin = tables(video_clock, 64)
    for first in range(0, HEADS, 4):
        ropes = rope_heads(
            [
                (key_in[:, head(h)].astype(jnp.float32), gain(4, h), vcos, vsin)
                for h in range(first, first + 4)
            ]
        )
        vk_send[:, first * HEAD_DIM : (first + 4) * HEAD_DIM] = jnp.concatenate(
            ropes, axis=1
        ).astype(jnp.bfloat16)

    for copy in input_copies[16:] + weight_copies:
        copy.wait()

    def project(chunks):
        products = [
            jnp.dot(hidden_in[...], wbuf[n], preferred_element_type=jnp.float32)
            for n in chunks
        ]
        ropes = rope_heads(
            [
                (products[i][:, head(part)], gain(5, 2 * n + part), vcos, vsin)
                for i, n in enumerate(chunks)
                for part in range(2)
            ]
        )
        for i, n in enumerate(chunks):
            vq_send[:, 256 * n : 256 * n + 256] = jnp.concatenate(
                ropes[2 * i : 2 * i + 2], axis=1
            ).astype(jnp.bfloat16)

    for chunks in ((0, 1), (2, 3), (4, 5)):
        project(chunks)

    own_rows = aligned(core * 256 + zh * 64, 64)
    own_lanes = aligned(zh * GW, 128)
    for d in (1, 3, 2):
        to = plus(zh, d)
        lanes = pl.ds(aligned(to * GW, 128), GW)
        target = device(cfg, x, to, y, core)
        start(vk_send.at[:, lanes], vk.at[pl.ds(own_rows, 64)], "zk", d - 1, target)
        start(video_value.at[0, :, lanes], vv.at[pl.ds(own_rows, 64)], "zv", d - 1, target)
    own_value = pltpu.make_async_copy(
        video_value.at[0, :, pl.ds(own_lanes, GW)], vv.at[pl.ds(own_rows, 64)], in_sem.at[18]
    )
    own_value.start()
    vk[pl.ds(own_rows, 64)] = vk_send[:, pl.ds(own_lanes, GW)]

    vq_rows = pl.ds(aligned(zh * 64, 64), 64)
    for d in (1, 3, 2):
        to = plus(zh, d)
        start(
            vq_send.at[:, pl.ds(aligned(to * GW, 128), GW)],
            vq.at[vq_rows],
            "zq",
            d - 1,
            device(cfg, x, to, y, core),
        )
    vq[vq_rows] = vq_send[:, pl.ds(own_lanes, GW)]

    def base_a(core_, x_, y_):
        return core_ * 512 + (y_ * 4 + x_) * 16

    def base_b(core_, x_, y_):
        return core_ * 512 + 256 + (x_ * 4 + y_) * 16

    def own(base, count):
        return pl.ds(aligned(base, 16), count)

    def rows_of(recv):
        received = [recv[z].astype(jnp.float32) for z in range(4)]

        def rows(k):
            return jnp.concatenate(
                [one[8 * k : 8 * k + 8] for one in received], axis=0
            ).astype(jnp.bfloat16)

        return [rows(k) for k in range(4)]

    def place(ref, core, lane, rows):
        lanes = slice(lane, lane + rows.shape[1])
        ref[own(base_a(core, x, y), 16), lanes] = rows[:16]
        ref[own(base_b(core, x, y), 16), lanes] = rows[16:]

    def first_phase(ref, name, core):
        mine_a = ref.at[own(base_a(core, x, y), 16)]
        mine_b = ref.at[own(base_b(core, x, y), 16)]
        for d in (1, 3, 2):
            start(
                mine_a, mine_a, name + "ax", d - 1, device(cfg, plus(x, d), zh, y, me)
            )
            start(
                mine_b, mine_b, name + "by", d - 1, device(cfg, x, zh, plus(y, d), me)
            )

    def second_phase(ref, name, core):
        for d in (1, 3, 2):
            arrived(
                ref.at[own(base_a(core, minus(x, d), y), 16)], name + "ax", d - 1
            )
            arrived(
                ref.at[own(base_b(core, x, minus(y, d)), 16)], name + "by", d - 1
            )
        row_a = ref.at[own(base_a(core, 0, y), 64)]
        row_b = ref.at[own(base_b(core, x, 0), 64)]
        for d in (1, 3, 2):
            start(
                row_a, row_a, name + "ay", d - 1, device(cfg, x, zh, plus(y, d), me)
            )
            start(
                row_b, row_b, name + "bx", d - 1, device(cfg, plus(x, d), zh, y, me)
            )

    def gathered(ref, name, core):
        for d in (1, 3, 2):
            arrived(ref.at[own(base_a(core, 0, minus(y, d)), 64)], name + "ay", d - 1)
            arrived(ref.at[own(base_b(core, minus(x, d), 0), 64)], name + "bx", d - 1)

    for d in (1, 3, 2):
        arrived(recv1.at[minus(zh, d)], "z1", d - 1)
    queries, keys, values, kept = rows_of(recv1)
    kept = kept[:, :HEAD_DIM]
    place(g0, 0, 0, queries)
    first_phase(g0, "g0", 0)
    place(g1, core, CK, keys)
    place(g1, core, CV, values)
    place(g1, core, KEEP, kept)
    first_phase(g1, "g1", core)

    for d in (1, 3, 2):
        arrived(recv2.at[minus(zh, d)], "z2", d - 1)
    queries, keys, values, _ = rows_of(recv2)
    srows = pl.ds(aligned(x * 32, 32), 32)
    squery[srows] = queries
    brows = pl.ds(aligned(core * 128 + y * 32, 32), 32)
    sblock[brows, CK : CK + GW] = keys
    sblock[brows, CV : CV + GW] = values
    sblock[brows, KEEP : KEEP + HEAD_DIM] = kept
    for d in (1, 3, 2):
        start(
            squery.at[srows], squery.at[srows], "sqx", d - 1, device(cfg, plus(x, d), zh, y, core)
        )
        start(
            sblock.at[brows], sblock.at[brows], "sky", d - 1, device(cfg, x, zh, plus(y, d), core)
        )

    second_phase(g0, "g0", 0)
    second_phase(g1, "g1", core)

    for d in (1, 3, 2):
        arrived(sblock.at[pl.ds(aligned(core * 128 + minus(y, d) * 32, 32), 32)], "sky", d - 1)
    mine = sblock.at[pl.ds(aligned(core * 128, 128), 128)]
    start(mine, mine, "sib", 3, sibling)
    for d in (1, 3, 2):
        arrived(squery.at[pl.ds(aligned(minus(x, d) * 32, 32), 32)], "sqx", d - 1)
    arrived(sblock.at[pl.ds(aligned(other * 128, 128), 128)], "sib", 3)

    def pack(put, results):
        lane = lax.broadcasted_iota(jnp.int32, results[0].shape, 1)
        lane = lane[:, :HEAD_DIM] // 16
        totals = jnp.zeros(lane.shape, jnp.float32)
        for h, both in enumerate(results):
            put(head(h), both[:, :HEAD_DIM].astype(jnp.bfloat16))
            total = both[:, HEAD_DIM:]
            high = total.astype(jnp.bfloat16).astype(jnp.float32)
            totals = jnp.where(lane == 2 * h, high, totals)
            totals = jnp.where(lane == 2 * h + 1, total - high, totals)
        put(slice(GW, SUM_LANES), totals.astype(jnp.bfloat16))

    def put_self(lanes, rows):
        spartial[:, lanes] = rows

    pack(
        put_self,
        [
            weigh(
                squery[:, head(h)],
                sblock[:, head(h, CK)],
                jnp.concatenate([sblock[:, head(h, CV)], sblock[:, KEEP:KV_LANES]], axis=1),
            )
            for h in range(GROUP)
        ],
    )
    for d in (1, 3, 2):
        px = plus(x, d)
        start(
            spartial.at[pl.ds(aligned(px * 32, 32), 32)],
            spartials.at[x],
            "ss",
            d - 1,
            device(cfg, px, zh, y, core),
        )
    spartials[x] = spartial[srows]

    own_value.wait()
    for d in (1, 3, 2):
        there = pl.ds(aligned(core * 256 + minus(zh, d) * 64, 64), 64)
        arrived(vk.at[there], "zk", d - 1)
        arrived(vv.at[there], "zv", d - 1)
    mine = pl.ds(aligned(core * 256, 256), 256)
    theirs = pl.ds(aligned(other * 256, 256), 256)
    start(vk.at[mine], vk.at[mine], "sib", 0, sibling)
    start(vv.at[mine], vv.at[mine], "sib", 1, sibling)

    gathered(g0, "g0", 0)

    arrived(vk.at[theirs], "sib", 0)
    arrived(vv.at[theirs], "sib", 1)
    ones = jnp.ones((512, HEAD_DIM), jnp.bfloat16)
    for pair in ((1, 3), (2, 0)):
        spots = []
        for dx in pair:
            px = plus(x, dx)
            for which in range(2):
                for py in range(4):
                    spots.append((px, py, which))

        def put(lanes, rows):
            for n, (px, py, which) in enumerate(spots):
                row = aligned((px * 4 + py) * 32 + 16 * which, 16)
                partial[pl.ds(row, 16), lanes] = rows[16 * n : 16 * n + 16]

        results = []
        for h in range(GROUP):
            queries = []
            for dx in pair:
                px = plus(x, dx)
                for py in range(4):
                    queries.append(g0[own(base_a(0, px, py), 16), head(h)])
                queries.append(g0[own(base_b(0, px, 0), 64), head(h)])
            results.append(
                weigh(
                    jnp.concatenate(queries, axis=0),
                    vk[:, head(h)],
                    jnp.concatenate([vv[:, head(h)], ones], axis=1),
                )
            )
        pack(put, results)
        for dx in pair:
            px = plus(x, dx)
            for dy in (1, 3, 2, 0):
                if dx or dy:
                    py = plus(y, dy)
                    start(
                        partial.at[pl.ds(aligned((px * 4 + py) * 32, 32), 32)],
                        partials.at[x * 4 + y],
                        "rs",
                        dx * 4 + dy,
                        device(cfg, px, zh, py, core),
                    )
    partials[x * 4 + y] = partial[pl.ds(aligned((x * 4 + y) * 32, 32), 32)]

    gathered(g1, "g1", core)
    mine = g1.at[pl.ds(aligned(core * 512, 512), 512)]
    start(mine, mine, "sib", 2, sibling)
    arrived(g1.at[pl.ds(aligned(other * 512, 512), 512)], "sib", 2)
    for d in (1, 3, 2):
        arrived(vq.at[pl.ds(aligned(minus(zh, d) * 64, 64), 64)], "zq", d - 1)

    is_final = cfg == zh // 2
    slot_out = cfg * 2 + lax.rem(zh, 2)
    final_cfg = zh // 2
    near_copies = []

    def final(src, dst, name, d):
        copy = remote(
            src,
            dst,
            FIRST[name] + d,
            FIRST[name] + slot_out,
            device(final_cfg, x, plus(zh, d), y, core),
        )
        if d:
            copy.start()
            sends.append(copy)
        else:
            pl.when(jnp.logical_not(is_final))(copy.start)
            near_copies.append(copy)

    for pair in ((1, 3), (2, 0)):
        rows = [aligned(plus(zh, d) * 64, 64) for d in pair]
        for h in range(GROUP):
            both = weigh(
                jnp.concatenate([vq[pl.ds(row, 64), head(h)] for row in rows], axis=0),
                g1[:, head(h, CK)],
                jnp.concatenate([g1[:, head(h, CV)], g1[:, KEEP:KV_LANES]], axis=1),
            )
            done = (both[:, :HEAD_DIM] / both[:, HEAD_DIM:]).astype(jnp.bfloat16)
            for n, row in enumerate(rows):
                vpart[pl.ds(row, 64), head(h)] = done[64 * n : 64 * n + 64]
        for d, row in zip(pair, rows):
            final(vpart.at[pl.ds(row, 64)], vfin.at[slot_out], "vf", d)

    for dx in (1, 3, 2, 0):
        for dy in (1, 3, 2, 0):
            if dx or dy:
                arrived(
                    partials.at[minus(x, dx) * 4 + minus(y, dy)], "rs", dx * 4 + dy
                )
    for d in (1, 3, 2):
        arrived(spartials.at[minus(x, d)], "ss", d - 1)

    def quotients(ref, count):
        summed = ref[0].astype(jnp.float32)
        for n in range(1, count):
            summed = summed + ref[n].astype(jnp.float32)
        result = []
        for h in range(GROUP):
            high = summed[:, GW + 32 * h : GW + 32 * h + 1]
            low = summed[:, GW + 32 * h + 16 : GW + 32 * h + 17]
            result.append(summed[:, head(h)] / (high + low))
        return jnp.concatenate(result, axis=1)

    part = quotients(spartials, 4) + quotients(partials, 16)
    apart[...] = part.astype(jnp.bfloat16).astype(jnp.float32)
    for d in (1, 3, 2, 0):
        row = aligned(plus(zh, d) * 8, 8)
        final(apart.at[pl.ds(row, 8)], afin.at[slot_out], "af", d)

    @pl.when(is_final)
    def _():
        own_copies = [
            pltpu.make_async_copy(
                vpart.at[pl.ds(aligned(zh * 64, 64), 64)], vfin.at[slot_out], in_sem.at[19]
            ),
            pltpu.make_async_copy(
                apart.at[pl.ds(aligned(zh * 8, 8), 8)], afin.at[slot_out], in_sem.at[20]
            ),
        ]
        for copy in own_copies:
            copy.start()
        for copy in own_copies:
            copy.wait()

    for fin, name in ((vfin, "vf"), (afin, "af")):
        for b in range(2):
            for j in range(2):
                here = jnp.logical_and(cfg == b, zh == 2 * cfg + j)

                @pl.when(jnp.logical_not(here))
                def _():
                    arrived(fin.at[2 * b + j], name, 2 * b + j)

    for copy in sends:
        copy.wait_send()

    @pl.when(jnp.logical_not(is_final))
    def _():
        for copy in near_copies:
            copy.wait_send()


def guide_kernel(video, audio, video_out, audio_out):
    def guide(cond, uncond):
        uncond = uncond.astype(jnp.float32)
        return (uncond + guide_scale * (cond.astype(jnp.float32) - uncond)).astype(
            jnp.bfloat16
        )

    for j in range(2):
        video_out[:, j * GW : (j + 1) * GW] = guide(video[j], video[2 + j])
    audio_out[...] = jnp.concatenate(
        [guide(audio[j], audio[2 + j]) for j in range(2)], axis=1
    )


def per_device(
    video_hidden,
    video_weight,
    video_key,
    video_value,
    audio_cross_key,
    audio_cross_value,
    audio_query,
    audio_self_query,
    audio_self_key,
    audio_self_value,
    v2a_qgain,
    v2a_kgain,
    self_qgain,
    self_kgain,
    a2v_qgain,
    a2v_kgain,
    video_time,
    audio_time,
    branch_keep,
):
    half_dim = HEAD_DIM // 2
    steps = np.arange(half_dim, dtype=np.float32) / np.float32(half_dim)
    frequencies = np.float32(rope_base) ** -steps
    frequencies = np.concatenate([frequencies, frequencies]).reshape(1, HEAD_DIM)

    vmem = pl.BlockSpec(memory_space=pltpu.VMEM)
    bf16, f32 = jnp.bfloat16, jnp.float32
    dma = pltpu.SemaphoreType.DMA
    hbm = pl.BlockSpec(memory_space=pltpu.HBM)
    parts = pl.pallas_call(
        kernel,
        out_shape=(
            jax.ShapeDtypeStruct((4, 64, GW), bf16),
            jax.ShapeDtypeStruct((4, 8, GW), f32),
        ),
        in_specs=[hbm] * 20,
        out_specs=(hbm, hbm),
        scratch_shapes=[
            pltpu.VMEM((64, 3072), bf16),
            pltpu.VMEM((64, 4 * GW), bf16),
            pltpu.VMEM((6, 8, 4 * GW), bf16),
            pltpu.VMEM((6, 4 * GW), f32),
            pltpu.VMEM((1, HEAD_DIM), f32),
            pltpu.SMEM((64,), jnp.int32),
            pltpu.SMEM((8,), jnp.int32),
            pltpu.SMEM((8,), jnp.int32),
            dma((21,)),
            pltpu.VMEM((6, 3072, 256), bf16),
            dma((6,)),
            pltpu.VMEM((4, 32, GW), bf16),
            pltpu.VMEM((4, 32, GW), bf16),
            pltpu.VMEM((4, 32, GW), bf16),
            pltpu.VMEM((4, 32, GW), bf16),
            pltpu.VMEM((512, GW), bf16),
            pltpu.VMEM((1024, KV_LANES), bf16),
            pltpu.VMEM((128, GW), bf16),
            pltpu.VMEM((256, KV_LANES), bf16),
            pltpu.VMEM((128, SUM_LANES), bf16),
            pltpu.VMEM((4, 32, SUM_LANES), bf16),
            pltpu.VMEM((64, 4 * GW), bf16),
            pltpu.VMEM((64, 4 * GW), bf16),
            pltpu.VMEM((256, GW), bf16),
            pltpu.VMEM((512, GW), bf16),
            pltpu.VMEM((512, GW), bf16),
            pltpu.VMEM((512, 512), bf16),
            pltpu.VMEM((16, 32, 512), bf16),
            pltpu.VMEM((256, GW), bf16),
            pltpu.VMEM((32, GW), f32),
            dma((SEMAPHORES,)),
            dma((SEMAPHORES,)),
        ],
        compiler_params=pltpu.CompilerParams(
            collective_id=0, has_side_effects=True, vmem_limit_bytes=64 * 1024 * 1024
        ),
        cost_estimate=pl.CostEstimate(
            flops=2 * 64 * 3072 * 1536 * 3, bytes_accessed=12_000_000, transcendentals=1_700_000
        ),
    )(
        video_hidden,
        video_weight,
        video_key,
        video_value,
        audio_cross_key,
        audio_cross_value,
        audio_query,
        audio_self_query,
        audio_self_key,
        audio_self_value,
        v2a_qgain,
        v2a_kgain,
        self_qgain,
        self_kgain,
        a2v_qgain,
        a2v_kgain,
        video_time,
        audio_time,
        branch_keep,
        frequencies,
    )
    return pl.pallas_call(
        guide_kernel,
        out_shape=(
            jax.ShapeDtypeStruct((64, 2 * GW), bf16),
            jax.ShapeDtypeStruct((8, 2 * GW), bf16),
        ),
        in_specs=[vmem, vmem],
        out_specs=(vmem, vmem),
    )(*parts)


def solution(mesh):
    in_specs = (
        P("cfg", "seq", None),
        P(),
        P("cfg", "seq", None),
        P("cfg", "seq", None),
        P("cfg", "seq", None),
        P("cfg", "seq", None),
        P("cfg", "seq", None),
        P("cfg", "seq", None),
        P("cfg", "seq", None),
        P("cfg", "seq", None),
        P(),
        P(),
        P(),
        P(),
        P(),
        P(),
        P("seq"),
        P("seq"),
        P("cfg", "seq"),
    )
    out_specs = (P("seq", "cfg"), P("seq", "cfg"))
    return jax.shard_map(
        per_device, mesh=mesh, in_specs=in_specs, out_specs=out_specs, check_vma=False
    )
```

```python
import math

import jax
import jax.numpy as jnp
import numpy as np
from jax import lax
from jax.experimental import pallas as pl
from jax.experimental.pallas import tpu as pltpu
from jax.sharding import PartitionSpec as P

HEADS = 12
HEAD_DIM = 128
MESH = pl.DeviceIdType.MESH

epsilon = 1e-06
rope_base = 10000.0
guide_scale = 3.0

GROUP = 3
GW = GROUP * HEAD_DIM
CK, CV, KEEP, KV_LANES = 0, 384, 768, 896
SCORE_SCALE = math.log2(math.e) / math.sqrt(HEAD_DIM)
NT = (((1,), (1,)), ((), ()))


def rope_heads(items):
    means = [jnp.mean(rows * rows, axis=1, keepdims=True) for rows, _, _, _ in items]
    scaled = [
        rows * lax.rsqrt(mean + epsilon) * gain
        for mean, (rows, gain, _, _) in zip(means, items)
    ]
    turned = [pltpu.roll(one, 64, 1) for one in scaled]
    return [
        one * cos + other * sin
        for one, other, (_, _, cos, sin) in zip(scaled, turned, items)
    ]


def weigh(queries, keys, values):
    scores = lax.dot_general(queries, keys, NT, preferred_element_type=jnp.float32)
    weights = jnp.exp2(scores * SCORE_SCALE).astype(jnp.bfloat16)
    return jnp.dot(weights, values, preferred_element_type=jnp.float32)


def head(index, base=0):
    return slice(base + index * HEAD_DIM, base + (index + 1) * HEAD_DIM)


TRANSFERS = (
    "z1",
    "z2",
    "zk",
    "zv",
    "zq",
    "g0ax",
    "g0by",
    "g0ay",
    "g0bx",
    "g1ax",
    "g1by",
    "g1ay",
    "g1bx",
    "sqx",
    "sky",
    "sib_k",
    "sib_v",
    "sib_s",
    "sib_g",
    "rs",
    "ss",
    "vf",
    "af",
    "vf_near",
    "af_near",
)
SEM = {name: n for n, name in enumerate(TRANSFERS)}


def kernel(
    hidden_hbm,
    weight,
    video_key_hbm,
    video_value,
    cross_key_hbm,
    cross_value_hbm,
    audio_query_hbm,
    self_query_hbm,
    self_key_hbm,
    self_value_hbm,
    v2a_qgain_hbm,
    v2a_kgain_hbm,
    self_qgain_hbm,
    self_kgain_hbm,
    a2v_qgain_hbm,
    a2v_kgain_hbm,
    video_time,
    audio_time,
    branch_keep,
    frequency,
    vfin,
    afin,
    hidden_in,
    key_in,
    audio_in,
    gain_in,
    frequency_in,
    video_clock,
    audio_clock,
    keep_in,
    in_sem,
    wbuf,
    stage1,
    stage2,
    recv1,
    recv2,
    g0,
    g1,
    squery,
    sblock,
    spartial,
    spartials,
    vq_send,
    vk_send,
    vq,
    vk,
    vv,
    partial,
    partials,
    vpart,
    apart,
    send_sem,
    recv_sem,
):
    cfg = lax.axis_index("cfg")
    seq = lax.axis_index("seq")
    core = lax.rem(seq, 2)
    y = lax.rem(seq // 2, 4)
    zh = lax.rem(seq // 8, 4)
    x = seq // 32

    def plus(value, d):
        return lax.rem(value + 4 + d, 4)

    def device(cfg_, x_, zh_, y_, core_):
        return (cfg_, ((x_ * 4 + zh_) * 4 + y_) * 2 + core_)

    def group_of(z):
        return lax.rem(z, 2) * 2 + z // 2

    def at(dx=0, dy=0, dz=0):
        return device(cfg, plus(x, dx), plus(zh, dz), plus(y, dy), core)

    sibling = device(cfg, x, zh, y, 1 - core)

    def remote(src, dst, name, target):
        return pltpu.make_async_remote_copy(
            src_ref=src,
            dst_ref=dst,
            send_sem=send_sem.at[SEM[name]],
            recv_sem=recv_sem.at[SEM[name]],
            device_id=target,
            device_id_type=MESH,
        )

    def start(src, dst, name, target):
        remote(src, dst, name, target).start()

    def arrived(ref, name):
        remote(ref, ref, name, sibling).wait_recv()

    def sent(ref, name):
        remote(ref, ref, name, sibling).wait_send()

    def rows(first, count):
        return pl.ds(first, count)

    barrier = pltpu.get_barrier_semaphore()
    peers = [sibling]
    for dx in range(4):
        for dy in range(4):
            if dx or dy:
                peers.append(at(dx=dx, dy=dy))
    for d in range(4):
        if d:
            peers.append(at(dz=d))
        peers.append(device(1 - cfg, x, plus(zh, d), y, core))
    for peer in peers:
        pl.semaphore_signal(barrier, inc=1, device_id=peer, device_id_type=MESH)

    first_inputs = [
        (audio_time, audio_clock, 0),
        (branch_keep.at[0], keep_in, 1),
        (frequency, frequency_in, 2),
        (a2v_qgain_hbm, gain_in.at[0], 3),
        (v2a_kgain_hbm, gain_in.at[1], 4),
    ]
    second_inputs = [(self_qgain_hbm, gain_in.at[2], 5), (self_kgain_hbm, gain_in.at[3], 6)]
    video_inputs = [
        (video_time, video_clock, 7),
        (video_key_hbm.at[0], key_in, 8),
        (a2v_kgain_hbm, gain_in.at[4], 9),
    ]
    query_inputs = [(v2a_qgain_hbm, gain_in.at[5], 10), (hidden_hbm.at[0], hidden_in, 11)]
    audio_inputs = [
        (audio_query_hbm.at[0], audio_in.at[0], 12),
        (cross_key_hbm.at[0], audio_in.at[1], 12),
        (cross_value_hbm.at[0], audio_in.at[2], 12),
        (self_query_hbm.at[0], audio_in.at[3], 13),
        (self_key_hbm.at[0], audio_in.at[4], 13),
        (self_value_hbm.at[0], audio_in.at[5], 13),
    ]

    def local(entry):
        src, dst, n = entry
        return pltpu.make_async_copy(src, dst, in_sem.at[n])

    for entry in first_inputs + audio_inputs + second_inputs + video_inputs + query_inputs:
        local(entry).start()

    for n in range(6):
        local((weight.at[:, pl.ds(n * 256, 256)], wbuf.at[n], 14)).start()

    def spread(scalars, count):
        row = lax.broadcasted_iota(jnp.int32, (8, HEAD_DIM), 0)
        tiles = []
        for first in range(0, count, 8):
            tile = jnp.zeros((8, HEAD_DIM), jnp.int32)
            for r in range(8):
                tile = jnp.where(row == r, scalars[first + r], tile)
            tiles.append(tile)
        return jnp.concatenate(tiles, axis=0).astype(jnp.float32)

    def tables(scalars, count):
        angles = spread(scalars, count) * frequency_in[...]
        lanes = lax.broadcasted_iota(jnp.int32, (count, HEAD_DIM), 1)
        sin = jnp.sin(angles)
        return jnp.cos(angles), jnp.where(lanes < HEAD_DIM // 2, -sin, sin)

    def gain(which, h):
        return gain_in[which, head(h)].reshape(1, HEAD_DIM)

    def audio_rows(which, h):
        return audio_in[which, :, head(h)].astype(jnp.float32)

    def wait_audio(group):
        three = audio_in.at[pl.ds(3 * group, 3)]
        local((three, three, 12 + group)).wait()

    for entry in first_inputs:
        local(entry).wait()
    wait_audio(0)
    acos, asin = tables(audio_clock, 8)
    mask = spread(keep_in, 8)
    nothing = jnp.zeros((8, HEAD_DIM), jnp.float32)

    def stage(ref, base, last):
        ropes = rope_heads(
            [
                (audio_rows(base + n, h), gain(base // 3 * 2 + n, h), acos, asin)
                for n in range(2)
                for h in range(HEADS)
            ]
        )
        values = [audio_rows(base + 2, h) * mask for h in range(HEADS)]
        for group in range(4):
            of = slice(group * GROUP, (group + 1) * GROUP)
            pieces = ropes[:HEADS][of] + ropes[HEADS:][of] + values[of] + [last]
            halves = [jnp.concatenate(pieces[n : n + 5], axis=1) for n in (0, 5)]
            ref[group] = jnp.concatenate(halves, axis=0).astype(jnp.bfloat16)

    stage(stage1, 0, mask)
    pl.semaphore_wait(barrier, len(peers))
    for d in (2, 1, 3):
        start(stage1.at[group_of(plus(zh, d))], recv1.at[d], "z1", at(dz=d))
    recv1[0] = stage1[group_of(zh)]

    for entry in second_inputs:
        local(entry).wait()
    wait_audio(1)
    stage(stage2, 3, nothing)
    for d in (2, 1, 3):
        start(stage2.at[group_of(plus(zh, d))], recv2.at[d], "z2", at(dz=d))
    recv2[0] = stage2[group_of(zh)]

    for entry in video_inputs:
        local(entry).wait()
    vcos, vsin = tables(video_clock, 64)
    for first in range(0, HEADS, 4):
        ropes = rope_heads(
            [
                (key_in[:, head(h)].astype(jnp.float32), gain(4, h), vcos, vsin)
                for h in range(first, first + 4)
            ]
        )
        vk_send[:, first * HEAD_DIM : (first + 4) * HEAD_DIM] = jnp.concatenate(
            ropes, axis=1
        ).astype(jnp.bfloat16)

    def lanes_of(z):
        return pl.ds(pl.multiple_of(group_of(z) * GW, 128), GW)

    for d in (2, 1, 3):
        start(vk_send.at[:, lanes_of(plus(zh, d))], vk.at[rows(64 * d, 64)], "zk", at(dz=d))
        start(
            video_value.at[0, :, lanes_of(plus(zh, d))], vv.at[rows(64 * d, 64)], "zv", at(dz=d)
        )
    own_value = local((video_value.at[0, :, lanes_of(zh)], vv.at[rows(0, 64)], 15))
    own_value.start()
    vk[0:64] = vk_send[:, lanes_of(zh)]

    for entry in query_inputs:
        local(entry).wait()
    local((wbuf, wbuf, 14)).wait()

    def project(chunks):
        products = [
            jnp.dot(hidden_in[...], wbuf[n], preferred_element_type=jnp.float32)
            for n in chunks
        ]
        ropes = rope_heads(
            [
                (products[i][:, head(part)], gain(5, 2 * n + part), vcos, vsin)
                for i, n in enumerate(chunks)
                for part in range(2)
            ]
        )
        for i, n in enumerate(chunks):
            vq_send[:, 256 * n : 256 * n + 256] = jnp.concatenate(
                ropes[2 * i : 2 * i + 2], axis=1
            ).astype(jnp.bfloat16)

    for chunks in ((0, 1), (2, 3), (4, 5)):
        project(chunks)
    vq[0:64] = vq_send[:, lanes_of(zh)]

    def rows_of(recv):
        received = [recv[d].astype(jnp.float32) for d in range(4)]

        def piece(n):
            row, lane = 8 * (n // 5), n % 5 * HEAD_DIM
            return jnp.concatenate(
                [one[row : row + 8, lane : lane + HEAD_DIM] for one in received], axis=0
            )

        pieces = [piece(n).astype(jnp.bfloat16) for n in range(10)]
        return [
            jnp.concatenate(pieces[n : n + GROUP], axis=1) for n in range(0, 9, GROUP)
        ] + pieces[9:]

    def place(ref, lane, block):
        lanes = slice(lane, lane + block.shape[1])
        ref[0:16, lanes] = block[:16]
        ref[256:272, lanes] = block[16:]

    def first_phase(ref, name):
        for d in (2, 1, 3):
            start(ref.at[rows(0, 16)], ref.at[rows(16 * d, 16)], name + "ax", at(dx=d))
            start(ref.at[rows(256, 16)], ref.at[rows(256 + 16 * d, 16)], name + "by", at(dy=d))

    def second_phase(ref, name):
        arrived(ref.at[rows(16, 48)], name + "ax")
        arrived(ref.at[rows(272, 48)], name + "by")
        for d in (2, 1, 3):
            start(ref.at[rows(0, 64)], ref.at[rows(64 * d, 64)], name + "ay", at(dy=d))
            start(ref.at[rows(256, 64)], ref.at[rows(256 + 64 * d, 64)], name + "bx", at(dx=d))

    def gathered(ref, name):
        arrived(ref.at[rows(64, 192)], name + "ay")
        arrived(ref.at[rows(320, 192)], name + "bx")

    arrived(recv1.at[rows(1, 3)], "z1")
    queries, keys, values, kept = rows_of(recv1)
    place(g0, 0, queries)
    first_phase(g0, "g0")
    place(g1, CK, keys)
    place(g1, CV, values)
    place(g1, KEEP, kept)
    first_phase(g1, "g1")

    arrived(recv2.at[rows(1, 3)], "z2")
    queries, keys, values, _ = rows_of(recv2)
    squery[0:32] = queries
    sblock[0:32, CK : CK + GW] = keys
    sblock[0:32, CV : CV + GW] = values
    sblock[0:32, KEEP : KEEP + HEAD_DIM] = kept
    for d in (2, 1, 3):
        start(squery.at[rows(0, 32)], squery.at[rows(32 * d, 32)], "sqx", at(dx=d))
        start(sblock.at[rows(0, 32)], sblock.at[rows(32 * d, 32)], "sky", at(dy=d))

    for d in (2, 1, 3):
        start(vq_send.at[:, lanes_of(plus(zh, d))], vq.at[rows(64 * d, 64)], "zq", at(dz=d))

    second_phase(g0, "g0")
    second_phase(g1, "g1")

    arrived(sblock.at[rows(32, 96)], "sky")
    start(sblock.at[rows(0, 128)], sblock.at[rows(128, 128)], "sib_s", sibling)

    lane = lax.broadcasted_iota(jnp.int32, (16, HEAD_DIM), 1)
    lane_group = lax.rem(lane, 64) // 8

    def pack(ref, slot, results, first, second):
        halves = []
        for start_row in (first, second):
            totals = jnp.zeros((16, HEAD_DIM), jnp.float32)
            for h, both in enumerate(results):
                total = both[start_row : start_row + 16, HEAD_DIM:]
                high = total.astype(jnp.bfloat16).astype(jnp.float32)
                totals = jnp.where(lane_group == 2 * h, high, totals)
                totals = jnp.where(lane_group == 2 * h + 1, total - high, totals)
            halves.append(totals)
        for h, both in enumerate(results):
            for n, start_row in enumerate((first, second)):
                ref[slot, 32 * h + 16 * n : 32 * h + 16 * n + 16] = both[
                    start_row : start_row + 16, :HEAD_DIM
                ].astype(jnp.bfloat16)
        ref[slot, 96:112] = jnp.where(lane < 64, halves[0], halves[1]).astype(jnp.bfloat16)

    own_value.wait()
    arrived(vk.at[rows(64, 192)], "zk")
    arrived(vv.at[rows(64, 192)], "zv")
    start(vk.at[rows(0, 256)], vk.at[rows(256, 256)], "sib_k", sibling)
    start(vv.at[rows(0, 256)], vv.at[rows(256, 256)], "sib_v", sibling)
    gathered(g0, "g0")
    ones = jnp.ones((256, HEAD_DIM), jnp.bfloat16)

    def audio_over_video(pair, h, first):
        queries = []
        for dx in pair:
            for dy in range(4):
                row = (4 * dy + dx) * 16
                queries.append(g0[row : row + 16, head(h)])
            row = 256 + 64 * dx
            queries.append(g0[row : row + 64, head(h)])
        return weigh(
            jnp.concatenate(queries, axis=0),
            vk[first : first + 256, head(h)],
            jnp.concatenate([vv[first : first + 256, head(h)], ones], axis=1),
        )

    pairs = ((2, 1), (3, 0))
    near = [[audio_over_video(pair, h, 0) for h in range(GROUP)] for pair in pairs]

    arrived(squery.at[rows(32, 96)], "sqx")
    arrived(sblock.at[rows(128, 128)], "sib_s")
    results = [
        weigh(
            squery[:, head(h)],
            sblock[:, head(h, CK)],
            jnp.concatenate([sblock[:, head(h, CV)], sblock[:, KEEP:KV_LANES]], axis=1),
        )
        for h in range(GROUP)
    ]
    for dx in (2, 1, 3, 0):
        if dx:
            pack(spartial, dx, results, 32 * dx, 32 * dx + 16)
            start(spartial.at[dx], spartials.at[dx], "ss", at(dx=-dx))
        else:
            pack(spartials, dx, results, 32 * dx, 32 * dx + 16)

    arrived(vk.at[rows(256, 256)], "sib_k")
    arrived(vv.at[rows(256, 256)], "sib_v")
    summed = [
        [near_results[h] + audio_over_video(pair, h, 256) for h in range(GROUP)]
        for pair, near_results in zip(pairs, near)
    ]
    for pair, results in zip(pairs, summed):
        for n, dx in enumerate(pair):
            for dy in (2, 1, 3, 0):
                slot = 4 * dx + dy
                row = 128 * n + 16 * dy
                if slot:
                    pack(partial, slot, results, row, row + 64)
                    start(partial.at[slot], partials.at[slot], "rs", at(dx=-dx, dy=-dy))
                else:
                    pack(partials, slot, results, row, row + 64)

    gathered(g1, "g1")
    start(g1.at[rows(0, 512)], g1.at[rows(512, 512)], "sib_g", sibling)
    arrived(vq.at[rows(64, 192)], "zq")

    def video_over_audio(pair, h, first):
        return weigh(
            jnp.concatenate([vq[64 * d : 64 * d + 64, head(h)] for d in pair], axis=0),
            g1[first : first + 512, head(h, CK)],
            jnp.concatenate(
                [g1[first : first + 512, head(h, CV)], g1[first : first + 512, KEEP:KV_LANES]],
                axis=1,
            ),
        )

    final_cfg = lax.rem(zh, 2)
    is_final = cfg == final_cfg
    slot_out = cfg * 2 + zh // 2

    def final(src, dst, name, d):
        target = device(final_cfg, x, plus(zh, -d), y, core)
        if d:
            start(src, dst, name, target)
        else:
            near_copy = pltpu.make_async_remote_copy(
                src_ref=src,
                dst_ref=dst,
                send_sem=send_sem.at[SEM[name + "_near"]],
                recv_sem=recv_sem.at[SEM[name]],
                device_id=target,
                device_id_type=MESH,
            )
            here_copy = pltpu.make_async_copy(src, dst, recv_sem.at[SEM[name]])
            pl.when(jnp.logical_not(is_final))(near_copy.start)
            pl.when(is_final)(here_copy.start)

    near = [[video_over_audio(pair, h, 0) for h in range(GROUP)] for pair in pairs]
    arrived(g1.at[rows(512, 512)], "sib_g")
    summed = [
        [near_results[h] + video_over_audio(pair, h, 512) for h in range(GROUP)]
        for pair, near_results in zip(pairs, near)
    ]
    for pair, results in zip(pairs, summed):
        for h, both in enumerate(results):
            done = (both[:, :HEAD_DIM] / both[:, HEAD_DIM:]).astype(jnp.bfloat16)
            for n, d in enumerate(pair):
                vpart[64 * d : 64 * d + 64, head(h)] = done[64 * n : 64 * n + 64]
        for d in pair:
            final(vpart.at[rows(64 * d, 64)], vfin.at[slot_out], "vf", d)

    def quotients(ref, count):
        summed = ref[0].astype(jnp.float32)
        for n in range(1, count):
            summed = summed + ref[n].astype(jnp.float32)
        tile = summed[96:112]
        result = []
        for h in range(GROUP):
            totals = [
                tile[:, first : first + 1] + tile[:, first + 8 : first + 9]
                for first in (16 * h, 64 + 16 * h)
            ]
            result.append(summed[32 * h : 32 * h + 32] / jnp.concatenate(totals, axis=0))
        return jnp.concatenate(result, axis=1)

    arrived(spartials.at[rows(1, 3)], "ss")
    self_part = quotients(spartials, 4)
    arrived(partials.at[rows(1, 15)], "rs")
    part = self_part + quotients(partials, 16)
    apart[...] = part.astype(jnp.bfloat16).astype(jnp.float32)
    for d in (2, 1, 3, 0):
        final(apart.at[rows(8 * d, 8)], afin.at[slot_out], "af", d)

    for name in ("z1", "z2"):
        sent(stage1.at[rows(0, 3)], name)
    for name in ("zk", "zv", "zq"):
        sent(vk.at[rows(0, 192)], name)
    for name, ref in (("g0", g0), ("g1", g1)):
        for kind, count in (("ax", 48), ("by", 48), ("ay", 192), ("bx", 192)):
            sent(ref.at[rows(0, count)], name + kind)
    sent(squery.at[rows(0, 96)], "sqx")
    sent(sblock.at[rows(0, 96)], "sky")
    sent(vk.at[rows(0, 256)], "sib_k")
    sent(vv.at[rows(0, 256)], "sib_v")
    sent(sblock.at[rows(0, 128)], "sib_s")
    sent(g1.at[rows(0, 512)], "sib_g")
    sent(partial.at[rows(1, 15)], "rs")
    sent(spartial.at[rows(1, 3)], "ss")
    sent(vpart.at[rows(64, 192)], "vf")
    sent(apart.at[rows(8, 24)], "af")

    @pl.when(jnp.logical_not(is_final))
    def _():
        sent(vpart.at[rows(0, 64)], "vf_near")
        sent(apart.at[rows(0, 8)], "af_near")

    arrived(vfin, "vf")
    arrived(afin, "af")


def guide_kernel(video, audio, video_out, audio_out):
    def guide(cond, uncond):
        uncond = uncond.astype(jnp.float32)
        return (uncond + guide_scale * (cond.astype(jnp.float32) - uncond)).astype(
            jnp.bfloat16
        )

    for j in range(2):
        video_out[:, j * GW : (j + 1) * GW] = guide(video[j], video[2 + j])
    audio_out[...] = jnp.concatenate(
        [guide(audio[j], audio[2 + j]) for j in range(2)], axis=1
    )


def per_device(
    video_hidden,
    video_weight,
    video_key,
    video_value,
    audio_cross_key,
    audio_cross_value,
    audio_query,
    audio_self_query,
    audio_self_key,
    audio_self_value,
    v2a_qgain,
    v2a_kgain,
    self_qgain,
    self_kgain,
    a2v_qgain,
    a2v_kgain,
    video_time,
    audio_time,
    branch_keep,
):
    half_dim = HEAD_DIM // 2
    steps = np.arange(half_dim, dtype=np.float32) / np.float32(half_dim)
    frequencies = np.float32(rope_base) ** -steps
    frequencies = np.concatenate([frequencies, frequencies]).reshape(1, HEAD_DIM)

    vmem = pl.BlockSpec(memory_space=pltpu.VMEM)
    bf16, f32 = jnp.bfloat16, jnp.float32
    dma = pltpu.SemaphoreType.DMA
    hbm = pl.BlockSpec(memory_space=pltpu.HBM)
    parts = pl.pallas_call(
        kernel,
        out_shape=(
            jax.ShapeDtypeStruct((4, 64, GW), bf16),
            jax.ShapeDtypeStruct((4, 8, GW), f32),
        ),
        in_specs=[hbm] * 20,
        out_specs=(hbm, hbm),
        scratch_shapes=[
            pltpu.VMEM((64, 3072), bf16),
            pltpu.VMEM((64, 4 * GW), bf16),
            pltpu.VMEM((6, 8, 4 * GW), bf16),
            pltpu.VMEM((6, 4 * GW), f32),
            pltpu.VMEM((1, HEAD_DIM), f32),
            pltpu.SMEM((64,), jnp.int32),
            pltpu.SMEM((8,), jnp.int32),
            pltpu.SMEM((8,), jnp.int32),
            dma((16,)),
            pltpu.VMEM((6, 3072, 256), bf16),
            pltpu.VMEM((4, 16, 5 * HEAD_DIM), bf16),
            pltpu.VMEM((4, 16, 5 * HEAD_DIM), bf16),
            pltpu.VMEM((4, 16, 5 * HEAD_DIM), bf16),
            pltpu.VMEM((4, 16, 5 * HEAD_DIM), bf16),
            pltpu.VMEM((512, GW), bf16),
            pltpu.VMEM((1024, KV_LANES), bf16),
            pltpu.VMEM((128, GW), bf16),
            pltpu.VMEM((256, KV_LANES), bf16),
            pltpu.VMEM((4, 112, HEAD_DIM), bf16),
            pltpu.VMEM((4, 112, HEAD_DIM), bf16),
            pltpu.VMEM((64, 4 * GW), bf16),
            pltpu.VMEM((64, 4 * GW), bf16),
            pltpu.VMEM((256, GW), bf16),
            pltpu.VMEM((512, GW), bf16),
            pltpu.VMEM((512, GW), bf16),
            pltpu.VMEM((16, 112, HEAD_DIM), bf16),
            pltpu.VMEM((16, 112, HEAD_DIM), bf16),
            pltpu.VMEM((256, GW), bf16),
            pltpu.VMEM((32, GW), f32),
            dma((len(TRANSFERS),)),
            dma((len(TRANSFERS),)),
        ],
        compiler_params=pltpu.CompilerParams(
            collective_id=0, has_side_effects=True, vmem_limit_bytes=64 * 1024 * 1024
        ),
        cost_estimate=pl.CostEstimate(
            flops=2 * 64 * 3072 * 1536 * 3, bytes_accessed=12_000_000, transcendentals=1_700_000
        ),
    )(
        video_hidden,
        video_weight,
        video_key,
        video_value,
        audio_cross_key,
        audio_cross_value,
        audio_query,
        audio_self_query,
        audio_self_key,
        audio_self_value,
        v2a_qgain,
        v2a_kgain,
        self_qgain,
        self_kgain,
        a2v_qgain,
        a2v_kgain,
        video_time,
        audio_time,
        branch_keep,
        frequencies,
    )
    return pl.pallas_call(
        guide_kernel,
        out_shape=(
            jax.ShapeDtypeStruct((64, 2 * GW), bf16),
            jax.ShapeDtypeStruct((8, 2 * GW), bf16),
        ),
        in_specs=[vmem, vmem],
        out_specs=(vmem, vmem),
    )(*parts)


def solution(mesh):
    in_specs = (
        P("cfg", "seq", None),
        P(),
        P("cfg", "seq", None),
        P("cfg", "seq", None),
        P("cfg", "seq", None),
        P("cfg", "seq", None),
        P("cfg", "seq", None),
        P("cfg", "seq", None),
        P("cfg", "seq", None),
        P("cfg", "seq", None),
        P(),
        P(),
        P(),
        P(),
        P(),
        P(),
        P("seq"),
        P("seq"),
        P("cfg", "seq"),
    )
    out_specs = (P("seq", "cfg"), P("seq", "cfg"))
    return jax.shard_map(
        per_device, mesh=mesh, in_specs=in_specs, out_specs=out_specs, check_vma=False
    )
```

```python
import math

import jax
import jax.numpy as jnp
import numpy as np
from jax import lax
from jax.experimental import pallas as pl
from jax.experimental.pallas import tpu as pltpu
from jax.sharding import PartitionSpec as P

HEADS = 12
HEAD_DIM = 128
MESH = pl.DeviceIdType.MESH

epsilon = 1e-06
rope_base = 10000.0
guide_scale = 3.0

GROUP = 3
GW = GROUP * HEAD_DIM
CK, CV, KEEP, KV_LANES = 0, 384, 768, 896
SCORE_SCALE = math.log2(math.e) / math.sqrt(HEAD_DIM)
NT = (((1,), (1,)), ((), ()))


def rope_heads(items):
    means = [jnp.mean(rows * rows, axis=1, keepdims=True) for rows, _, _, _ in items]
    scaled = [
        rows * lax.rsqrt(mean + epsilon) * gain
        for mean, (rows, gain, _, _) in zip(means, items)
    ]
    turned = [pltpu.roll(one, 64, 1) for one in scaled]
    return [
        one * cos + other * sin
        for one, other, (_, _, cos, sin) in zip(scaled, turned, items)
    ]


def weigh(queries, keys, values):
    scores = lax.dot_general(queries, keys, NT, preferred_element_type=jnp.float32)
    weights = jnp.exp2(scores * SCORE_SCALE).astype(jnp.bfloat16)
    return jnp.dot(weights, values, preferred_element_type=jnp.float32)


def head(index, base=0):
    return slice(base + index * HEAD_DIM, base + (index + 1) * HEAD_DIM)


TRANSFERS = (
    "z1",
    "z2",
    "zk",
    "zv",
    "zq",
    "g0",
    "g1ax",
    "g1by",
    "g1ay",
    "g1bx",
    "sqx",
    "sky",
    "sib_k",
    "sib_v",
    "sib_s",
    "sib_g",
    "rs",
    "ss",
    "vf",
    "af",
    "vf_near",
    "af_near",
)
SEM = {name: n for n, name in enumerate(TRANSFERS)}


def kernel(
    hidden_hbm,
    weight,
    video_key_hbm,
    video_value,
    cross_key_hbm,
    cross_value_hbm,
    audio_query_hbm,
    self_query_hbm,
    self_key_hbm,
    self_value_hbm,
    v2a_qgain_hbm,
    v2a_kgain_hbm,
    self_qgain_hbm,
    self_kgain_hbm,
    a2v_qgain_hbm,
    a2v_kgain_hbm,
    video_time,
    audio_time,
    branch_keep,
    frequency,
    vfin,
    afin,
    hidden_in,
    key_in,
    audio_in,
    gain_in,
    frequency_in,
    video_clock,
    audio_clock,
    keep_in,
    in_sem,
    wbuf,
    stage1,
    stage2,
    recv1,
    recv2,
    g0,
    g1,
    squery,
    sblock,
    spartial,
    spartials,
    vq_send,
    vk_send,
    vq,
    vk,
    vv,
    partial,
    partials,
    vpart,
    apart,
    send_sem,
    recv_sem,
):
    cfg = lax.axis_index("cfg")
    seq = lax.axis_index("seq")
    core = lax.rem(seq, 2)
    y = lax.rem(seq // 2, 4)
    zh = lax.rem(seq // 8, 4)
    x = seq // 32

    def plus(value, d):
        return lax.rem(value + 4 + d, 4)

    def device(cfg_, x_, zh_, y_, core_):
        return (cfg_, ((x_ * 4 + zh_) * 4 + y_) * 2 + core_)

    def group_of(z):
        return lax.rem(z, 2) * 2 + z // 2

    def at(dx=0, dy=0, dz=0):
        return device(cfg, plus(x, dx), plus(zh, dz), plus(y, dy), core)

    sibling = device(cfg, x, zh, y, 1 - core)

    def remote(src, dst, name, target):
        return pltpu.make_async_remote_copy(
            src_ref=src,
            dst_ref=dst,
            send_sem=send_sem.at[SEM[name]],
            recv_sem=recv_sem.at[SEM[name]],
            device_id=target,
            device_id_type=MESH,
        )

    def start(src, dst, name, target):
        remote(src, dst, name, target).start()

    def arrived(ref, name):
        remote(ref, ref, name, sibling).wait_recv()

    def sent(ref, name):
        remote(ref, ref, name, sibling).wait_send()

    def rows(first, count):
        return pl.ds(first, count)

    barrier = pltpu.get_barrier_semaphore()
    peers = [sibling]
    for dx in range(4):
        for dy in range(4):
            if dx or dy:
                peers.append(at(dx=dx, dy=dy))
    for d in range(4):
        if d:
            peers.append(at(dz=d))
        peers.append(device(1 - cfg, x, plus(zh, d), y, core))
    for peer in peers:
        pl.semaphore_signal(barrier, inc=1, device_id=peer, device_id_type=MESH)

    first_inputs = [
        (audio_time, audio_clock, 0),
        (branch_keep.at[0], keep_in, 1),
        (frequency, frequency_in, 2),
        (a2v_qgain_hbm, gain_in.at[0], 3),
        (v2a_kgain_hbm, gain_in.at[1], 4),
    ]
    second_inputs = [(self_qgain_hbm, gain_in.at[2], 5), (self_kgain_hbm, gain_in.at[3], 6)]
    video_inputs = [
        (video_time, video_clock, 7),
        (video_key_hbm.at[0], key_in, 8),
        (a2v_kgain_hbm, gain_in.at[4], 9),
    ]
    query_inputs = [(v2a_qgain_hbm, gain_in.at[5], 10), (hidden_hbm.at[0], hidden_in, 11)]
    audio_inputs = [
        (audio_query_hbm.at[0], audio_in.at[0], 12),
        (cross_key_hbm.at[0], audio_in.at[1], 12),
        (cross_value_hbm.at[0], audio_in.at[2], 12),
        (self_query_hbm.at[0], audio_in.at[3], 13),
        (self_key_hbm.at[0], audio_in.at[4], 13),
        (self_value_hbm.at[0], audio_in.at[5], 13),
    ]

    def local(entry):
        src, dst, n = entry
        return pltpu.make_async_copy(src, dst, in_sem.at[n])

    for entry in first_inputs + audio_inputs + second_inputs + video_inputs + query_inputs:
        local(entry).start()

    for n in range(6):
        local((weight.at[:, pl.ds(n * 256, 256)], wbuf.at[n], 14)).start()

    def spread(scalars, count):
        row = lax.broadcasted_iota(jnp.int32, (8, HEAD_DIM), 0)
        tiles = []
        for first in range(0, count, 8):
            tile = jnp.zeros((8, HEAD_DIM), jnp.int32)
            for r in range(8):
                tile = jnp.where(row == r, scalars[first + r], tile)
            tiles.append(tile)
        return jnp.concatenate(tiles, axis=0).astype(jnp.float32)

    def tables(scalars, count):
        angles = spread(scalars, count) * frequency_in[...]
        lanes = lax.broadcasted_iota(jnp.int32, (count, HEAD_DIM), 1)
        sin = jnp.sin(angles)
        return jnp.cos(angles), jnp.where(lanes < HEAD_DIM // 2, -sin, sin)

    def gain(which, h):
        return gain_in[which, head(h)].reshape(1, HEAD_DIM)

    def audio_rows(which, h):
        return audio_in[which, :, head(h)].astype(jnp.float32)

    def wait_audio(group):
        three = audio_in.at[pl.ds(3 * group, 3)]
        local((three, three, 12 + group)).wait()

    for entry in first_inputs:
        local(entry).wait()
    wait_audio(0)
    acos, asin = tables(audio_clock, 8)
    mask = spread(keep_in, 8)
    nothing = jnp.zeros((8, HEAD_DIM), jnp.float32)

    def stage(ref, base, last):
        ropes = rope_heads(
            [
                (audio_rows(base + n, h), gain(base // 3 * 2 + n, h), acos, asin)
                for n in range(2)
                for h in range(HEADS)
            ]
        )
        values = [audio_rows(base + 2, h) * mask for h in range(HEADS)]
        for group in range(4):
            of = slice(group * GROUP, (group + 1) * GROUP)
            pieces = ropes[:HEADS][of] + ropes[HEADS:][of] + values[of] + [last]
            halves = [jnp.concatenate(pieces[n : n + 5], axis=1) for n in (0, 5)]
            ref[group] = jnp.concatenate(halves, axis=0).astype(jnp.bfloat16)

    stage(stage1, 0, mask)
    pl.semaphore_wait(barrier, len(peers))
    for d in (2, 1, 3):
        start(stage1.at[group_of(plus(zh, d))], recv1.at[d], "z1", at(dz=d))
    recv1[0] = stage1[group_of(zh)]

    for entry in second_inputs:
        local(entry).wait()
    wait_audio(1)
    stage(stage2, 3, nothing)
    for d in (2, 1, 3):
        start(stage2.at[group_of(plus(zh, d))], recv2.at[d], "z2", at(dz=d))
    recv2[0] = stage2[group_of(zh)]

    for entry in video_inputs:
        local(entry).wait()
    vcos, vsin = tables(video_clock, 64)
    for first in range(0, HEADS, 4):
        ropes = rope_heads(
            [
                (key_in[:, head(h)].astype(jnp.float32), gain(4, h), vcos, vsin)
                for h in range(first, first + 4)
            ]
        )
        vk_send[:, first * HEAD_DIM : (first + 4) * HEAD_DIM] = jnp.concatenate(
            ropes, axis=1
        ).astype(jnp.bfloat16)

    def lanes_of(z):
        return pl.ds(pl.multiple_of(group_of(z) * GW, 128), GW)

    def send_keys_values():
        for d in (2, 1, 3):
            start(vk_send.at[:, lanes_of(plus(zh, d))], vk.at[rows(64 * d, 64)], "zk", at(dz=d))
            start(
                video_value.at[0, :, lanes_of(plus(zh, d))], vv.at[rows(64 * d, 64)], "zv", at(dz=d)
            )

    pl.when(core == 0)(send_keys_values)
    own_value = local((video_value.at[0, :, lanes_of(zh)], vv.at[rows(0, 64)], 15))
    own_value.start()
    vk[0:64] = vk_send[:, lanes_of(zh)]

    for entry in query_inputs:
        local(entry).wait()
    local((wbuf, wbuf, 14)).wait()

    def project(chunks):
        products = [
            jnp.dot(hidden_in[...], wbuf[n], preferred_element_type=jnp.float32)
            for n in chunks
        ]
        ropes = rope_heads(
            [
                (products[i][:, head(part)], gain(5, 2 * n + part), vcos, vsin)
                for i, n in enumerate(chunks)
                for part in range(2)
            ]
        )
        for i, n in enumerate(chunks):
            vq_send[:, 256 * n : 256 * n + 256] = jnp.concatenate(
                ropes[2 * i : 2 * i + 2], axis=1
            ).astype(jnp.bfloat16)

    for chunks in ((0, 1), (2, 3), (4, 5)):
        project(chunks)
    pl.when(core == 1)(send_keys_values)
    vq[0:64] = vq_send[:, lanes_of(zh)]

    def rows_of(recv):
        received = [recv[d].astype(jnp.float32) for d in range(4)]

        def piece(n):
            row, lane = 8 * (n // 5), n % 5 * HEAD_DIM
            return jnp.concatenate(
                [one[row : row + 8, lane : lane + HEAD_DIM] for one in received], axis=0
            )

        pieces = [piece(n).astype(jnp.bfloat16) for n in range(10)]
        return [
            jnp.concatenate(pieces[n : n + GROUP], axis=1) for n in range(0, 9, GROUP)
        ] + pieces[9:]

    def place(ref, lane, block):
        lanes = slice(lane, lane + block.shape[1])
        ref[0:16, lanes] = block[:16]
        ref[256:272, lanes] = block[16:]

    def first_phase(ref, name):
        for d in (2, 1, 3):
            start(ref.at[rows(0, 16)], ref.at[rows(16 * d, 16)], name + "ax", at(dx=d))
            start(ref.at[rows(256, 16)], ref.at[rows(256 + 16 * d, 16)], name + "by", at(dy=d))

    def second_phase(ref, name):
        arrived(ref.at[rows(16, 48)], name + "ax")
        arrived(ref.at[rows(272, 48)], name + "by")
        for d in (2, 1, 3):
            start(ref.at[rows(0, 64)], ref.at[rows(64 * d, 64)], name + "ay", at(dy=d))
            start(ref.at[rows(256, 64)], ref.at[rows(256 + 64 * d, 64)], name + "bx", at(dx=d))

    def gathered(ref, name):
        arrived(ref.at[rows(64, 192)], name + "ay")
        arrived(ref.at[rows(320, 192)], name + "bx")

    arrived(recv1.at[rows(1, 3)], "z1")
    queries, keys, values, kept = rows_of(recv1)
    place(g1, CK, keys)
    place(g1, CV, values)
    place(g1, KEEP, kept)
    first_phase(g1, "g1")
    g0[0:32] = queries
    for dx in (2, 1, 3, 0):
        for dy in (2, 1, 3, 0):
            if dx or dy:
                start(
                    g0.at[rows(0, 32)],
                    g0.at[rows(32 * (4 * dx + dy), 32)],
                    "g0",
                    at(dx=dx, dy=dy),
                )

    arrived(recv2.at[rows(1, 3)], "z2")
    queries, keys, values, _ = rows_of(recv2)
    squery[0:32] = queries
    sblock[0:32, CK : CK + GW] = keys
    sblock[0:32, CV : CV + GW] = values
    sblock[0:32, KEEP : KEEP + HEAD_DIM] = kept
    for d in (2, 1, 3):
        start(squery.at[rows(0, 32)], squery.at[rows(32 * d, 32)], "sqx", at(dx=d))
        start(sblock.at[rows(0, 32)], sblock.at[rows(32 * d, 32)], "sky", at(dy=d))

    second_phase(g1, "g1")

    for d in (2, 1, 3):
        start(vq_send.at[:, lanes_of(plus(zh, d))], vq.at[rows(64 * d, 64)], "zq", at(dz=d))

    lane = lax.broadcasted_iota(jnp.int32, (16, HEAD_DIM), 1)
    lane_group = lax.rem(lane, 64) // 8

    def pack(ref, slot, results, first, second):
        halves = []
        for start_row in (first, second):
            totals = jnp.zeros((16, HEAD_DIM), jnp.float32)
            for h, both in enumerate(results):
                total = both[start_row : start_row + 16, HEAD_DIM:]
                high = total.astype(jnp.bfloat16).astype(jnp.float32)
                totals = jnp.where(lane_group == 2 * h, high, totals)
                totals = jnp.where(lane_group == 2 * h + 1, total - high, totals)
            halves.append(totals)
        for h, both in enumerate(results):
            for n, start_row in enumerate((first, second)):
                ref[slot, 32 * h + 16 * n : 32 * h + 16 * n + 16] = both[
                    start_row : start_row + 16, :HEAD_DIM
                ].astype(jnp.bfloat16)
        ref[slot, 96:112] = jnp.where(lane < 64, halves[0], halves[1]).astype(jnp.bfloat16)

    own_value.wait()
    arrived(vk.at[rows(64, 192)], "zk")
    arrived(vv.at[rows(64, 192)], "zv")
    start(vk.at[rows(0, 256)], vk.at[rows(256, 256)], "sib_k", sibling)
    start(vv.at[rows(0, 256)], vv.at[rows(256, 256)], "sib_v", sibling)
    arrived(g0.at[rows(32, 480)], "g0")
    ones = jnp.ones((256, HEAD_DIM), jnp.bfloat16)

    def audio_over_video(pair, h, first):
        queries = [g0[128 * dx : 128 * dx + 128, head(h)] for dx in pair]
        return weigh(
            jnp.concatenate(queries, axis=0),
            vk[first : first + 256, head(h)],
            jnp.concatenate([vv[first : first + 256, head(h)], ones], axis=1),
        )

    pairs = ((2, 1), (3, 0))
    near = [[audio_over_video(pair, h, 0) for h in range(GROUP)] for pair in pairs]

    arrived(vk.at[rows(256, 256)], "sib_k")
    arrived(vv.at[rows(256, 256)], "sib_v")
    summed = [
        [near_results[h] + audio_over_video(pair, h, 256) for h in range(GROUP)]
        for pair, near_results in zip(pairs, near)
    ]
    for pair, results in zip(pairs, summed):
        for n, dx in enumerate(pair):
            for dy in (2, 1, 3, 0):
                slot = 4 * dx + dy
                row = 128 * n + 32 * dy
                if slot:
                    pack(partial, slot, results, row, row + 16)
                    start(partial.at[slot], partials.at[slot], "rs", at(dx=-dx, dy=-dy))
                else:
                    pack(partials, slot, results, row, row + 16)

    arrived(sblock.at[rows(32, 96)], "sky")
    start(sblock.at[rows(0, 128)], sblock.at[rows(128, 128)], "sib_s", sibling)

    gathered(g1, "g1")
    start(g1.at[rows(0, 512)], g1.at[rows(512, 512)], "sib_g", sibling)
    arrived(vq.at[rows(64, 192)], "zq")

    def video_over_audio(pair, h, first):
        return weigh(
            jnp.concatenate([vq[64 * d : 64 * d + 64, head(h)] for d in pair], axis=0),
            g1[first : first + 512, head(h, CK)],
            jnp.concatenate(
                [g1[first : first + 512, head(h, CV)], g1[first : first + 512, KEEP:KV_LANES]],
                axis=1,
            ),
        )

    final_cfg = lax.rem(zh, 2)
    is_final = cfg == final_cfg
    slot_out = cfg * 2 + zh // 2

    def final(src, dst, name, d):
        target = device(final_cfg, x, plus(zh, -d), y, core)
        if d:
            start(src, dst, name, target)
        else:
            near_copy = pltpu.make_async_remote_copy(
                src_ref=src,
                dst_ref=dst,
                send_sem=send_sem.at[SEM[name + "_near"]],
                recv_sem=recv_sem.at[SEM[name]],
                device_id=target,
                device_id_type=MESH,
            )
            here_copy = pltpu.make_async_copy(src, dst, recv_sem.at[SEM[name]])
            pl.when(jnp.logical_not(is_final))(near_copy.start)
            pl.when(is_final)(here_copy.start)

    near = [[video_over_audio(pair, h, 0) for h in range(GROUP)] for pair in pairs]
    arrived(squery.at[rows(32, 96)], "sqx")
    arrived(sblock.at[rows(128, 128)], "sib_s")
    results = [
        weigh(
            squery[:, head(h)],
            sblock[:, head(h, CK)],
            jnp.concatenate([sblock[:, head(h, CV)], sblock[:, KEEP:KV_LANES]], axis=1),
        )
        for h in range(GROUP)
    ]
    for dx in (2, 1, 3, 0):
        if dx:
            pack(spartial, dx, results, 32 * dx, 32 * dx + 16)
            start(spartial.at[dx], spartials.at[dx], "ss", at(dx=-dx))
        else:
            pack(spartials, dx, results, 32 * dx, 32 * dx + 16)

    arrived(g1.at[rows(512, 512)], "sib_g")
    summed = [
        [near_results[h] + video_over_audio(pair, h, 512) for h in range(GROUP)]
        for pair, near_results in zip(pairs, near)
    ]
    for pair, results in zip(pairs, summed):
        for h, both in enumerate(results):
            done = (both[:, :HEAD_DIM] / both[:, HEAD_DIM:]).astype(jnp.bfloat16)
            for n, d in enumerate(pair):
                vpart[64 * d : 64 * d + 64, head(h)] = done[64 * n : 64 * n + 64]
        for d in pair:
            final(vpart.at[rows(64 * d, 64)], vfin.at[slot_out], "vf", d)

    def quotients(ref, count):
        summed = ref[0].astype(jnp.float32)
        for n in range(1, count):
            summed = summed + ref[n].astype(jnp.float32)
        tile = summed[96:112]
        result = []
        for h in range(GROUP):
            totals = [
                tile[:, first : first + 1] + tile[:, first + 8 : first + 9]
                for first in (16 * h, 64 + 16 * h)
            ]
            result.append(summed[32 * h : 32 * h + 32] / jnp.concatenate(totals, axis=0))
        return jnp.concatenate(result, axis=1)

    arrived(spartials.at[rows(1, 3)], "ss")
    self_part = quotients(spartials, 4)
    arrived(partials.at[rows(1, 15)], "rs")
    part = self_part + quotients(partials, 16)
    apart[...] = part.astype(jnp.bfloat16).astype(jnp.float32)
    for d in (2, 1, 3, 0):
        final(apart.at[rows(8 * d, 8)], afin.at[slot_out], "af", d)

    for name in ("z1", "z2"):
        sent(stage1.at[rows(0, 3)], name)
    for name in ("zk", "zv", "zq"):
        sent(vk.at[rows(0, 192)], name)
    sent(g0.at[rows(32, 480)], "g0")
    for kind, count in (("ax", 48), ("by", 48), ("ay", 192), ("bx", 192)):
        sent(g1.at[rows(0, count)], "g1" + kind)
    sent(squery.at[rows(0, 96)], "sqx")
    sent(sblock.at[rows(0, 96)], "sky")
    sent(vk.at[rows(0, 256)], "sib_k")
    sent(vv.at[rows(0, 256)], "sib_v")
    sent(sblock.at[rows(0, 128)], "sib_s")
    sent(g1.at[rows(0, 512)], "sib_g")
    sent(partial.at[rows(1, 15)], "rs")
    sent(spartial.at[rows(1, 3)], "ss")
    sent(vpart.at[rows(64, 192)], "vf")
    sent(apart.at[rows(8, 24)], "af")

    @pl.when(jnp.logical_not(is_final))
    def _():
        sent(vpart.at[rows(0, 64)], "vf_near")
        sent(apart.at[rows(0, 8)], "af_near")

    arrived(vfin, "vf")
    arrived(afin, "af")


def guide_kernel(video, audio, video_out, audio_out):
    def guide(cond, uncond):
        uncond = uncond.astype(jnp.float32)
        return (uncond + guide_scale * (cond.astype(jnp.float32) - uncond)).astype(
            jnp.bfloat16
        )

    for j in range(2):
        video_out[:, j * GW : (j + 1) * GW] = guide(video[j], video[2 + j])
    audio_out[...] = jnp.concatenate(
        [guide(audio[j], audio[2 + j]) for j in range(2)], axis=1
    )


def per_device(
    video_hidden,
    video_weight,
    video_key,
    video_value,
    audio_cross_key,
    audio_cross_value,
    audio_query,
    audio_self_query,
    audio_self_key,
    audio_self_value,
    v2a_qgain,
    v2a_kgain,
    self_qgain,
    self_kgain,
    a2v_qgain,
    a2v_kgain,
    video_time,
    audio_time,
    branch_keep,
):
    half_dim = HEAD_DIM // 2
    steps = np.arange(half_dim, dtype=np.float32) / np.float32(half_dim)
    frequencies = np.float32(rope_base) ** -steps
    frequencies = np.concatenate([frequencies, frequencies]).reshape(1, HEAD_DIM)

    vmem = pl.BlockSpec(memory_space=pltpu.VMEM)
    bf16, f32 = jnp.bfloat16, jnp.float32
    dma = pltpu.SemaphoreType.DMA
    hbm = pl.BlockSpec(memory_space=pltpu.HBM)
    parts = pl.pallas_call(
        kernel,
        out_shape=(
            jax.ShapeDtypeStruct((4, 64, GW), bf16),
            jax.ShapeDtypeStruct((4, 8, GW), f32),
        ),
        in_specs=[hbm] * 20,
        out_specs=(hbm, hbm),
        scratch_shapes=[
            pltpu.VMEM((64, 3072), bf16),
            pltpu.VMEM((64, 4 * GW), bf16),
            pltpu.VMEM((6, 8, 4 * GW), bf16),
            pltpu.VMEM((6, 4 * GW), f32),
            pltpu.VMEM((1, HEAD_DIM), f32),
            pltpu.SMEM((64,), jnp.int32),
            pltpu.SMEM((8,), jnp.int32),
            pltpu.SMEM((8,), jnp.int32),
            dma((16,)),
            pltpu.VMEM((6, 3072, 256), bf16),
            pltpu.VMEM((4, 16, 5 * HEAD_DIM), bf16),
            pltpu.VMEM((4, 16, 5 * HEAD_DIM), bf16),
            pltpu.VMEM((4, 16, 5 * HEAD_DIM), bf16),
            pltpu.VMEM((4, 16, 5 * HEAD_DIM), bf16),
            pltpu.VMEM((512, GW), bf16),
            pltpu.VMEM((1024, KV_LANES), bf16),
            pltpu.VMEM((128, GW), bf16),
            pltpu.VMEM((256, KV_LANES), bf16),
            pltpu.VMEM((4, 112, HEAD_DIM), bf16),
            pltpu.VMEM((4, 112, HEAD_DIM), bf16),
            pltpu.VMEM((64, 4 * GW), bf16),
            pltpu.VMEM((64, 4 * GW), bf16),
            pltpu.VMEM((256, GW), bf16),
            pltpu.VMEM((512, GW), bf16),
            pltpu.VMEM((512, GW), bf16),
            pltpu.VMEM((16, 112, HEAD_DIM), bf16),
            pltpu.VMEM((16, 112, HEAD_DIM), bf16),
            pltpu.VMEM((256, GW), bf16),
            pltpu.VMEM((32, GW), f32),
            dma((len(TRANSFERS),)),
            dma((len(TRANSFERS),)),
        ],
        compiler_params=pltpu.CompilerParams(
            collective_id=0, has_side_effects=True, vmem_limit_bytes=64 * 1024 * 1024
        ),
        cost_estimate=pl.CostEstimate(
            flops=2 * 64 * 3072 * 1536 * 3, bytes_accessed=12_000_000, transcendentals=1_700_000
        ),
    )(
        video_hidden,
        video_weight,
        video_key,
        video_value,
        audio_cross_key,
        audio_cross_value,
        audio_query,
        audio_self_query,
        audio_self_key,
        audio_self_value,
        v2a_qgain,
        v2a_kgain,
        self_qgain,
        self_kgain,
        a2v_qgain,
        a2v_kgain,
        video_time,
        audio_time,
        branch_keep,
        frequencies,
    )
    return pl.pallas_call(
        guide_kernel,
        out_shape=(
            jax.ShapeDtypeStruct((64, 2 * GW), bf16),
            jax.ShapeDtypeStruct((8, 2 * GW), bf16),
        ),
        in_specs=[vmem, vmem],
        out_specs=(vmem, vmem),
    )(*parts)


def solution(mesh):
    in_specs = (
        P("cfg", "seq", None),
        P(),
        P("cfg", "seq", None),
        P("cfg", "seq", None),
        P("cfg", "seq", None),
        P("cfg", "seq", None),
        P("cfg", "seq", None),
        P("cfg", "seq", None),
        P("cfg", "seq", None),
        P("cfg", "seq", None),
        P(),
        P(),
        P(),
        P(),
        P(),
        P(),
        P("seq"),
        P("seq"),
        P("cfg", "seq"),
    )
    out_specs = (P("seq", "cfg"), P("seq", "cfg"))
    return jax.shard_map(
        per_device, mesh=mesh, in_specs=in_specs, out_specs=out_specs, check_vma=False
    )
```

```python
import math

import jax
import jax.numpy as jnp
import numpy as np
from jax import lax
from jax.experimental import pallas as pl
from jax.experimental.pallas import tpu as pltpu
from jax.sharding import PartitionSpec as P

HEADS = 12
HEAD_DIM = 128
MESH = pl.DeviceIdType.MESH

epsilon = 1e-06
rope_base = 10000.0
guide_scale = 3.0

GROUP = 3
GW = GROUP * HEAD_DIM
CK, CV, KEEP, KV_LANES = 0, 384, 768, 896
SCORE_SCALE = math.log2(math.e) / math.sqrt(HEAD_DIM)
NT = (((1,), (1,)), ((), ()))


def rope_heads(items):
    means = [jnp.mean(rows * rows, axis=1, keepdims=True) for rows, _, _, _ in items]
    scaled = [
        rows * lax.rsqrt(mean + epsilon) * gain
        for mean, (rows, gain, _, _) in zip(means, items)
    ]
    turned = [pltpu.roll(one, 64, 1) for one in scaled]
    return [
        one * cos + other * sin
        for one, other, (_, _, cos, sin) in zip(scaled, turned, items)
    ]


def weigh(queries, keys, values):
    scores = lax.dot_general(queries, keys, NT, preferred_element_type=jnp.float32)
    weights = jnp.exp2(scores * SCORE_SCALE).astype(jnp.bfloat16)
    return jnp.dot(weights, values, preferred_element_type=jnp.float32)


def head(index, base=0):
    return slice(base + index * HEAD_DIM, base + (index + 1) * HEAD_DIM)


TRANSFERS = (
    "z1",
    "z2",
    "zk",
    "zv",
    "zq",
    "g0",
    "g1ax",
    "g1by",
    "g1ay",
    "g1bx",
    "sqx",
    "sky",
    "sib_k",
    "sib_v",
    "sib_s",
    "sib_g",
    "rs",
    "ss",
    "vf",
    "af",
    "vf_near",
    "af_near",
)
SEM = {name: n for n, name in enumerate(TRANSFERS)}


def kernel(
    hidden_hbm,
    weight,
    video_key_hbm,
    video_value,
    cross_key_hbm,
    cross_value_hbm,
    audio_query_hbm,
    self_query_hbm,
    self_key_hbm,
    self_value_hbm,
    v2a_qgain_hbm,
    v2a_kgain_hbm,
    self_qgain_hbm,
    self_kgain_hbm,
    a2v_qgain_hbm,
    a2v_kgain_hbm,
    video_time,
    audio_time,
    branch_keep,
    frequency,
    vfin,
    afin,
    hidden_in,
    key_in,
    audio_in,
    gain_in,
    frequency_in,
    video_clock,
    audio_clock,
    keep_in,
    in_sem,
    wbuf,
    stage1,
    stage2,
    recv1,
    recv2,
    g0,
    g1,
    squery,
    sblock,
    spartial,
    spartials,
    vq_send,
    vk_send,
    vq,
    vk,
    vv,
    partial,
    partials,
    vpart,
    apart,
    send_sem,
    recv_sem,
):
    cfg = lax.axis_index("cfg")
    seq = lax.axis_index("seq")
    core = lax.rem(seq, 2)
    y = lax.rem(seq // 2, 4)
    zh = lax.rem(seq // 8, 4)
    x = seq // 32

    def plus(value, d):
        return lax.rem(value + 4 + d, 4)

    def device(cfg_, x_, zh_, y_, core_):
        return (cfg_, ((x_ * 4 + zh_) * 4 + y_) * 2 + core_)

    def group_of(z):
        return lax.rem(z, 2) * 2 + z // 2

    def at(dx=0, dy=0, dz=0):
        return device(cfg, plus(x, dx), plus(zh, dz), plus(y, dy), core)

    sibling = device(cfg, x, zh, y, 1 - core)

    def remote(src, dst, name, target):
        return pltpu.make_async_remote_copy(
            src_ref=src,
            dst_ref=dst,
            send_sem=send_sem.at[SEM[name]],
            recv_sem=recv_sem.at[SEM[name]],
            device_id=target,
            device_id_type=MESH,
        )

    def start(src, dst, name, target):
        remote(src, dst, name, target).start()

    def arrived(ref, name):
        remote(ref, ref, name, sibling).wait_recv()

    def sent(ref, name):
        remote(ref, ref, name, sibling).wait_send()

    def rows(first, count):
        return pl.ds(first, count)

    barrier = pltpu.get_barrier_semaphore()
    peers = [sibling]
    for far in range(1, 5):
        for dx in range(4):
            for dy in range(4):
                if min(dx, 4 - dx) + min(dy, 4 - dy) == far:
                    peers.append(at(dx=dx, dy=dy))
    for d in (0, 1, 3, 2):
        if d:
            peers.append(at(dz=d))
        peers.append(device(1 - cfg, x, plus(zh, d), y, core))
    for peer in peers:
        pl.semaphore_signal(barrier, inc=1, device_id=peer, device_id_type=MESH)

    first_inputs = [
        (audio_time, audio_clock, 0),
        (branch_keep.at[0], keep_in, 1),
        (frequency, frequency_in, 2),
        (a2v_qgain_hbm, gain_in.at[0], 3),
        (v2a_kgain_hbm, gain_in.at[1], 4),
    ]
    second_inputs = [(self_qgain_hbm, gain_in.at[2], 5), (self_kgain_hbm, gain_in.at[3], 6)]
    video_inputs = [
        (video_time, video_clock, 7),
        (video_key_hbm.at[0], key_in, 8),
        (a2v_kgain_hbm, gain_in.at[4], 9),
    ]
    query_inputs = [(v2a_qgain_hbm, gain_in.at[5], 10), (hidden_hbm.at[0], hidden_in, 11)]
    audio_inputs = [
        (audio_query_hbm.at[0], audio_in.at[0], 12),
        (cross_key_hbm.at[0], audio_in.at[1], 12),
        (cross_value_hbm.at[0], audio_in.at[2], 12),
        (self_query_hbm.at[0], audio_in.at[3], 13),
        (self_key_hbm.at[0], audio_in.at[4], 13),
        (self_value_hbm.at[0], audio_in.at[5], 13),
    ]

    def local(entry):
        src, dst, n = entry
        return pltpu.make_async_copy(src, dst, in_sem.at[n])

    for entry in first_inputs + audio_inputs + second_inputs + video_inputs + query_inputs:
        local(entry).start()

    for n in range(6):
        local((weight.at[:, pl.ds(n * 256, 256)], wbuf.at[n], 14)).start()

    def spread(scalars, count):
        row = lax.broadcasted_iota(jnp.int32, (8, HEAD_DIM), 0)
        tiles = []
        for first in range(0, count, 8):
            tile = jnp.zeros((8, HEAD_DIM), jnp.int32)
            for r in range(8):
                tile = jnp.where(row == r, scalars[first + r], tile)
            tiles.append(tile)
        return jnp.concatenate(tiles, axis=0).astype(jnp.float32)

    def tables(scalars, count):
        angles = spread(scalars, count) * frequency_in[...]
        lanes = lax.broadcasted_iota(jnp.int32, (count, HEAD_DIM), 1)
        sin = jnp.sin(angles)
        return jnp.cos(angles), jnp.where(lanes < HEAD_DIM // 2, -sin, sin)

    def gain(which, h):
        return gain_in[which, head(h)].reshape(1, HEAD_DIM)

    def audio_rows(which, h):
        return audio_in[which, :, head(h)].astype(jnp.float32)

    def wait_audio(group):
        three = audio_in.at[pl.ds(3 * group, 3)]
        local((three, three, 12 + group)).wait()

    for entry in first_inputs:
        local(entry).wait()
    wait_audio(0)
    acos, asin = tables(audio_clock, 8)
    mask = spread(keep_in, 8)
    nothing = jnp.zeros((8, HEAD_DIM), jnp.float32)

    def stage(ref, base, last):
        ropes = rope_heads(
            [
                (audio_rows(base + n, h), gain(base // 3 * 2 + n, h), acos, asin)
                for n in range(2)
                for h in range(HEADS)
            ]
        )
        values = [audio_rows(base + 2, h) * mask for h in range(HEADS)]
        for group in range(4):
            of = slice(group * GROUP, (group + 1) * GROUP)
            pieces = ropes[:HEADS][of] + ropes[HEADS:][of] + values[of] + [last]
            halves = [jnp.concatenate(pieces[n : n + 5], axis=1) for n in (0, 5)]
            ref[group] = jnp.concatenate(halves, axis=0).astype(jnp.bfloat16)

    stage(stage1, 0, mask)
    pl.semaphore_wait(barrier, len(peers))
    for d in (2, 1, 3):
        start(stage1.at[group_of(plus(zh, d))], recv1.at[d], "z1", at(dz=d))
    recv1[0] = stage1[group_of(zh)]

    for entry in second_inputs:
        local(entry).wait()
    wait_audio(1)
    stage(stage2, 3, nothing)
    for d in (2, 1, 3):
        start(stage2.at[group_of(plus(zh, d))], recv2.at[d], "z2", at(dz=d))
    recv2[0] = stage2[group_of(zh)]

    for entry in video_inputs:
        local(entry).wait()
    vcos, vsin = tables(video_clock, 64)
    for first in range(0, HEADS, 4):
        ropes = rope_heads(
            [
                (key_in[:, head(h)].astype(jnp.float32), gain(4, h), vcos, vsin)
                for h in range(first, first + 4)
            ]
        )
        vk_send[:, first * HEAD_DIM : (first + 4) * HEAD_DIM] = jnp.concatenate(
            ropes, axis=1
        ).astype(jnp.bfloat16)

    def lanes_of(z):
        return pl.ds(pl.multiple_of(group_of(z) * GW, 128), GW)

    def send_keys_values():
        for d in (2, 1, 3):
            start(vk_send.at[:, lanes_of(plus(zh, d))], vk.at[rows(64 * d, 64)], "zk", at(dz=d))
            start(
                video_value.at[0, :, lanes_of(plus(zh, d))], vv.at[rows(64 * d, 64)], "zv", at(dz=d)
            )

    pl.when(core == 0)(send_keys_values)
    own_value = local((video_value.at[0, :, lanes_of(zh)], vv.at[rows(0, 64)], 15))
    own_value.start()
    vk[0:64] = vk_send[:, lanes_of(zh)]

    for entry in query_inputs:
        local(entry).wait()
    local((wbuf, wbuf, 14)).wait()

    def project(chunks):
        products = [
            jnp.dot(hidden_in[...], wbuf[n], preferred_element_type=jnp.float32)
            for n in chunks
        ]
        ropes = rope_heads(
            [
                (products[i][:, head(part)], gain(5, 2 * n + part), vcos, vsin)
                for i, n in enumerate(chunks)
                for part in range(2)
            ]
        )
        for i, n in enumerate(chunks):
            vq_send[:, 256 * n : 256 * n + 256] = jnp.concatenate(
                ropes[2 * i : 2 * i + 2], axis=1
            ).astype(jnp.bfloat16)

    for chunks in ((0, 1), (2, 3), (4, 5)):
        project(chunks)
    pl.when(core == 1)(send_keys_values)
    vq[0:64] = vq_send[:, lanes_of(zh)]

    def rows_of(recv):
        received = [recv[d].astype(jnp.float32) for d in range(4)]

        def piece(n):
            row, lane = 8 * (n // 5), n % 5 * HEAD_DIM
            return jnp.concatenate(
                [one[row : row + 8, lane : lane + HEAD_DIM] for one in received], axis=0
            )

        pieces = [piece(n).astype(jnp.bfloat16) for n in range(10)]
        return [
            jnp.concatenate(pieces[n : n + GROUP], axis=1) for n in range(0, 9, GROUP)
        ] + pieces[9:]

    def place(ref, lane, block):
        lanes = slice(lane, lane + block.shape[1])
        ref[0:16, lanes] = block[:16]
        ref[256:272, lanes] = block[16:]

    def first_phase(ref, name):
        for d in (2, 1, 3):
            start(ref.at[rows(0, 16)], ref.at[rows(16 * d, 16)], name + "ax", at(dx=d))
            start(ref.at[rows(256, 16)], ref.at[rows(256 + 16 * d, 16)], name + "by", at(dy=d))

    def second_phase(ref, name):
        arrived(ref.at[rows(16, 48)], name + "ax")
        arrived(ref.at[rows(272, 48)], name + "by")
        for d in (2, 1, 3):
            start(ref.at[rows(0, 64)], ref.at[rows(64 * d, 64)], name + "ay", at(dy=d))
            start(ref.at[rows(256, 64)], ref.at[rows(256 + 64 * d, 64)], name + "bx", at(dx=d))

    def gathered(ref, name):
        arrived(ref.at[rows(64, 192)], name + "ay")
        arrived(ref.at[rows(320, 192)], name + "bx")

    arrived(recv1.at[rows(1, 3)], "z1")
    queries, keys, values, kept = rows_of(recv1)
    place(g1, CK, keys)
    place(g1, CV, values)
    place(g1, KEEP, kept)
    first_phase(g1, "g1")
    g0[0:32] = queries
    for dx in (2, 1, 3, 0):
        for dy in (2, 1, 3, 0):
            if dx or dy:
                start(
                    g0.at[rows(0, 32)],
                    g0.at[rows(32 * (4 * dx + dy), 32)],
                    "g0",
                    at(dx=dx, dy=dy),
                )

    arrived(recv2.at[rows(1, 3)], "z2")
    queries, keys, values, _ = rows_of(recv2)
    squery[0:32] = queries
    sblock[0:32, CK : CK + GW] = keys
    sblock[0:32, CV : CV + GW] = values
    sblock[0:32, KEEP : KEEP + HEAD_DIM] = kept
    for d in (2, 1, 3):
        start(squery.at[rows(0, 32)], squery.at[rows(32 * d, 32)], "sqx", at(dx=d))
        start(sblock.at[rows(0, 32)], sblock.at[rows(32 * d, 32)], "sky", at(dy=d))

    second_phase(g1, "g1")

    for d in (2, 1, 3):
        start(vq_send.at[:, lanes_of(plus(zh, d))], vq.at[rows(64 * d, 64)], "zq", at(dz=d))

    lane = lax.broadcasted_iota(jnp.int32, (16, HEAD_DIM), 1)
    lane_group = lax.rem(lane, 64) // 8

    def pack(ref, slot, results, first, second):
        halves = []
        for start_row in (first, second):
            totals = jnp.zeros((16, HEAD_DIM), jnp.float32)
            for h, both in enumerate(results):
                total = both[start_row : start_row + 16, HEAD_DIM:]
                high = total.astype(jnp.bfloat16).astype(jnp.float32)
                totals = jnp.where(lane_group == 2 * h, high, totals)
                totals = jnp.where(lane_group == 2 * h + 1, total - high, totals)
            halves.append(totals)
        for h, both in enumerate(results):
            for n, start_row in enumerate((first, second)):
                ref[slot, 32 * h + 16 * n : 32 * h + 16 * n + 16] = both[
                    start_row : start_row + 16, :HEAD_DIM
                ].astype(jnp.bfloat16)
        ref[slot, 96:112] = jnp.where(lane < 64, halves[0], halves[1]).astype(jnp.bfloat16)

    own_value.wait()
    arrived(vk.at[rows(64, 192)], "zk")
    arrived(vv.at[rows(64, 192)], "zv")
    start(vk.at[rows(0, 256)], vk.at[rows(256, 256)], "sib_k", sibling)
    start(vv.at[rows(0, 256)], vv.at[rows(256, 256)], "sib_v", sibling)
    arrived(g0.at[rows(32, 480)], "g0")
    ones = jnp.ones((256, HEAD_DIM), jnp.bfloat16)

    def audio_over_video(pair, h, first):
        queries = [g0[128 * dx : 128 * dx + 128, head(h)] for dx in pair]
        return weigh(
            jnp.concatenate(queries, axis=0),
            vk[first : first + 256, head(h)],
            jnp.concatenate([vv[first : first + 256, head(h)], ones], axis=1),
        )

    pairs = ((2, 1), (3, 0))
    near = [[audio_over_video(pair, h, 0) for h in range(GROUP)] for pair in pairs]

    arrived(vk.at[rows(256, 256)], "sib_k")
    arrived(vv.at[rows(256, 256)], "sib_v")
    for pair, near_results in zip(pairs, near):
        results = [
            near_results[h] + audio_over_video(pair, h, 256) for h in range(GROUP)
        ]
        for n, dx in enumerate(pair):
            for dy in (2, 1, 3, 0):
                slot = 4 * dx + dy
                row = 128 * n + 32 * dy
                if slot:
                    pack(partial, slot, results, row, row + 16)
                    start(partial.at[slot], partials.at[slot], "rs", at(dx=-dx, dy=-dy))
                else:
                    pack(partials, slot, results, row, row + 16)

    arrived(sblock.at[rows(32, 96)], "sky")
    start(sblock.at[rows(0, 128)], sblock.at[rows(128, 128)], "sib_s", sibling)

    gathered(g1, "g1")
    start(g1.at[rows(0, 512)], g1.at[rows(512, 512)], "sib_g", sibling)
    arrived(vq.at[rows(64, 192)], "zq")

    def video_over_audio(pair, h, first):
        return weigh(
            jnp.concatenate([vq[64 * d : 64 * d + 64, head(h)] for d in pair], axis=0),
            g1[first : first + 512, head(h, CK)],
            jnp.concatenate(
                [g1[first : first + 512, head(h, CV)], g1[first : first + 512, KEEP:KV_LANES]],
                axis=1,
            ),
        )

    final_cfg = lax.rem(zh, 2)
    is_final = cfg == final_cfg
    slot_out = cfg * 2 + zh // 2

    def final(src, dst, name, d):
        target = device(final_cfg, x, plus(zh, -d), y, core)
        if d:
            start(src, dst, name, target)
        else:
            near_copy = pltpu.make_async_remote_copy(
                src_ref=src,
                dst_ref=dst,
                send_sem=send_sem.at[SEM[name + "_near"]],
                recv_sem=recv_sem.at[SEM[name]],
                device_id=target,
                device_id_type=MESH,
            )
            here_copy = pltpu.make_async_copy(src, dst, recv_sem.at[SEM[name]])
            pl.when(jnp.logical_not(is_final))(near_copy.start)
            pl.when(is_final)(here_copy.start)

    near = [[video_over_audio(pair, h, 0) for h in range(GROUP)] for pair in pairs]
    arrived(squery.at[rows(32, 96)], "sqx")
    arrived(sblock.at[rows(128, 128)], "sib_s")
    results = [
        weigh(
            squery[:, head(h)],
            sblock[:, head(h, CK)],
            jnp.concatenate([sblock[:, head(h, CV)], sblock[:, KEEP:KV_LANES]], axis=1),
        )
        for h in range(GROUP)
    ]
    for dx in (2, 1, 3, 0):
        if dx:
            pack(spartial, dx, results, 32 * dx, 32 * dx + 16)
            start(spartial.at[dx], spartials.at[dx], "ss", at(dx=-dx))
        else:
            pack(spartials, dx, results, 32 * dx, 32 * dx + 16)

    arrived(g1.at[rows(512, 512)], "sib_g")
    summed = [
        [near_results[h] + video_over_audio(pair, h, 512) for h in range(GROUP)]
        for pair, near_results in zip(pairs, near)
    ]
    for pair, results in zip(pairs, summed):
        for h, both in enumerate(results):
            done = (both[:, :HEAD_DIM] / both[:, HEAD_DIM:]).astype(jnp.bfloat16)
            for n, d in enumerate(pair):
                vpart[64 * d : 64 * d + 64, head(h)] = done[64 * n : 64 * n + 64]
        for d in pair:
            final(vpart.at[rows(64 * d, 64)], vfin.at[slot_out], "vf", d)

    def quotients(ref, count):
        summed = ref[0].astype(jnp.float32)
        for n in range(1, count):
            summed = summed + ref[n].astype(jnp.float32)
        tile = summed[96:112]
        result = []
        for h in range(GROUP):
            totals = [
                tile[:, first : first + 1] + tile[:, first + 8 : first + 9]
                for first in (16 * h, 64 + 16 * h)
            ]
            result.append(summed[32 * h : 32 * h + 32] / jnp.concatenate(totals, axis=0))
        return jnp.concatenate(result, axis=1)

    arrived(spartials.at[rows(1, 3)], "ss")
    self_part = quotients(spartials, 4)
    arrived(partials.at[rows(1, 15)], "rs")
    part = self_part + quotients(partials, 16)
    apart[...] = part.astype(jnp.bfloat16).astype(jnp.float32)
    for d in (2, 1, 3, 0):
        final(apart.at[rows(8 * d, 8)], afin.at[slot_out], "af", d)

    for name in ("z1", "z2"):
        sent(stage1.at[rows(0, 3)], name)
    for name in ("zk", "zv", "zq"):
        sent(vk.at[rows(0, 192)], name)
    sent(g0.at[rows(32, 480)], "g0")
    for kind, count in (("ax", 48), ("by", 48), ("ay", 192), ("bx", 192)):
        sent(g1.at[rows(0, count)], "g1" + kind)
    sent(squery.at[rows(0, 96)], "sqx")
    sent(sblock.at[rows(0, 96)], "sky")
    sent(vk.at[rows(0, 256)], "sib_k")
    sent(vv.at[rows(0, 256)], "sib_v")
    sent(sblock.at[rows(0, 128)], "sib_s")
    sent(g1.at[rows(0, 512)], "sib_g")
    sent(partial.at[rows(1, 15)], "rs")
    sent(spartial.at[rows(1, 3)], "ss")
    sent(vpart.at[rows(64, 192)], "vf")
    sent(apart.at[rows(8, 24)], "af")

    @pl.when(jnp.logical_not(is_final))
    def _():
        sent(vpart.at[rows(0, 64)], "vf_near")
        sent(apart.at[rows(0, 8)], "af_near")

    arrived(vfin, "vf")
    arrived(afin, "af")


def guide_kernel(video, audio, video_out, audio_out):
    def guide(cond, uncond):
        uncond = uncond.astype(jnp.float32)
        return (uncond + guide_scale * (cond.astype(jnp.float32) - uncond)).astype(
            jnp.bfloat16
        )

    for j in range(2):
        video_out[:, j * GW : (j + 1) * GW] = guide(video[j], video[2 + j])
    audio_out[...] = jnp.concatenate(
        [guide(audio[j], audio[2 + j]) for j in range(2)], axis=1
    )


def per_device(
    video_hidden,
    video_weight,
    video_key,
    video_value,
    audio_cross_key,
    audio_cross_value,
    audio_query,
    audio_self_query,
    audio_self_key,
    audio_self_value,
    v2a_qgain,
    v2a_kgain,
    self_qgain,
    self_kgain,
    a2v_qgain,
    a2v_kgain,
    video_time,
    audio_time,
    branch_keep,
):
    half_dim = HEAD_DIM // 2
    steps = np.arange(half_dim, dtype=np.float32) / np.float32(half_dim)
    frequencies = np.float32(rope_base) ** -steps
    frequencies = np.concatenate([frequencies, frequencies]).reshape(1, HEAD_DIM)

    vmem = pl.BlockSpec(memory_space=pltpu.VMEM)
    bf16, f32 = jnp.bfloat16, jnp.float32
    dma = pltpu.SemaphoreType.DMA
    hbm = pl.BlockSpec(memory_space=pltpu.HBM)
    parts = pl.pallas_call(
        kernel,
        out_shape=(
            jax.ShapeDtypeStruct((4, 64, GW), bf16),
            jax.ShapeDtypeStruct((4, 8, GW), f32),
        ),
        in_specs=[hbm] * 20,
        out_specs=(hbm, hbm),
        scratch_shapes=[
            pltpu.VMEM((64, 3072), bf16),
            pltpu.VMEM((64, 4 * GW), bf16),
            pltpu.VMEM((6, 8, 4 * GW), bf16),
            pltpu.VMEM((6, 4 * GW), f32),
            pltpu.VMEM((1, HEAD_DIM), f32),
            pltpu.SMEM((64,), jnp.int32),
            pltpu.SMEM((8,), jnp.int32),
            pltpu.SMEM((8,), jnp.int32),
            dma((16,)),
            pltpu.VMEM((6, 3072, 256), bf16),
            pltpu.VMEM((4, 16, 5 * HEAD_DIM), bf16),
            pltpu.VMEM((4, 16, 5 * HEAD_DIM), bf16),
            pltpu.VMEM((4, 16, 5 * HEAD_DIM), bf16),
            pltpu.VMEM((4, 16, 5 * HEAD_DIM), bf16),
            pltpu.VMEM((512, GW), bf16),
            pltpu.VMEM((1024, KV_LANES), bf16),
            pltpu.VMEM((128, GW), bf16),
            pltpu.VMEM((256, KV_LANES), bf16),
            pltpu.VMEM((4, 112, HEAD_DIM), bf16),
            pltpu.VMEM((4, 112, HEAD_DIM), bf16),
            pltpu.VMEM((64, 4 * GW), bf16),
            pltpu.VMEM((64, 4 * GW), bf16),
            pltpu.VMEM((256, GW), bf16),
            pltpu.VMEM((512, GW), bf16),
            pltpu.VMEM((512, GW), bf16),
            pltpu.VMEM((16, 112, HEAD_DIM), bf16),
            pltpu.VMEM((16, 112, HEAD_DIM), bf16),
            pltpu.VMEM((256, GW), bf16),
            pltpu.VMEM((32, GW), f32),
            dma((len(TRANSFERS),)),
            dma((len(TRANSFERS),)),
        ],
        compiler_params=pltpu.CompilerParams(
            collective_id=0, has_side_effects=True, vmem_limit_bytes=64 * 1024 * 1024
        ),
        cost_estimate=pl.CostEstimate(
            flops=2 * 64 * 3072 * 1536 * 3, bytes_accessed=12_000_000, transcendentals=1_700_000
        ),
    )(
        video_hidden,
        video_weight,
        video_key,
        video_value,
        audio_cross_key,
        audio_cross_value,
        audio_query,
        audio_self_query,
        audio_self_key,
        audio_self_value,
        v2a_qgain,
        v2a_kgain,
        self_qgain,
        self_kgain,
        a2v_qgain,
        a2v_kgain,
        video_time,
        audio_time,
        branch_keep,
        frequencies,
    )
    return pl.pallas_call(
        guide_kernel,
        out_shape=(
            jax.ShapeDtypeStruct((64, 2 * GW), bf16),
            jax.ShapeDtypeStruct((8, 2 * GW), bf16),
        ),
        in_specs=[vmem, vmem],
        out_specs=(vmem, vmem),
    )(*parts)


def solution(mesh):
    in_specs = (
        P("cfg", "seq", None),
        P(),
        P("cfg", "seq", None),
        P("cfg", "seq", None),
        P("cfg", "seq", None),
        P("cfg", "seq", None),
        P("cfg", "seq", None),
        P("cfg", "seq", None),
        P("cfg", "seq", None),
        P("cfg", "seq", None),
        P(),
        P(),
        P(),
        P(),
        P(),
        P(),
        P("seq"),
        P("seq"),
        P("cfg", "seq"),
    )
    out_specs = (P("seq", "cfg"), P("seq", "cfg"))
    return jax.shard_map(
        per_device, mesh=mesh, in_specs=in_specs, out_specs=out_specs, check_vma=False
    )
```
